256 devices in a mesh: row: 8 (over z), col: 32 (over y, x, core).
Axes of the slice: x: 4, y: 4, z: 8, core: 2. Of those that a mesh axis runs over, the one named last changes fastest.
Arguments:
- features: bfloat16 [131072, 128], P(('row', 'col')), may hold values from -6 to 6
- block_rows: int32 [8, 32, 64], P('row', 'col'), may hold values from 0 to 127
- block_cols: int32 [8, 32, 64], P('row', 'col'), may hold values from 0 to 31
- block_values: bfloat16 [8, 32, 64, 128, 128], P('row', 'col'), may hold values from -0.125 to 0.125
- weight_one: bfloat16 [128, 256], replicated, may hold values from -0.5 to 0.5
- bias_one: float32 [256], replicated, may hold values from -3 to 3
- weight_two: bfloat16 [256, 256], replicated, may hold values from -0.375 to 0.375
- bias_two: float32 [256], replicated, may hold values from -3 to 3
Outputs:
- hidden_two: bfloat16 [131072, 256], P(('row', 'col'))
The draws below stay inside these ranges and needn't reach their ends.
All inputs are finite; a program needn't handle non-finite values.
Results may differ from the reference program's by a relative error of at most 0.0065.
Values may be sent and summed in bfloat16 or wider, within the bound.
A program may use at most 128 MiB of HBM per device.

```python
import jax
import jax.numpy as jnp
from jax import lax

BS = 128
F_IN = 128
HID = 256
BLK_DEV = 4
NNZ = 64
NBLK = 1024
NODES = 131072
N_ROW = 8
N_COL = 32


def set_ends(values, key, least, top_value):
    index_at = [jax.random.randint(jax.random.fold_in(key, axis), (), 0, length) for axis, length in enumerate(values.shape)]
    main_axis = values.shape.index(max(values.shape))
    next_to = index_at[:main_axis] + [(index_at[main_axis] + 1) % values.shape[main_axis]] + index_at[main_axis + 1:]
    return values.at[tuple(index_at)].set(least).at[tuple(next_to)].set(top_value)


def block_scale(rng, dims, cuts, least, high):
    factor_of = 1.0
    for axis_at, blocks in cuts:
        steps = jax.random.uniform(jax.random.fold_in(jax.random.fold_in(rng, 6), axis_at), (blocks,), jnp.float32, least / len(cuts), high / len(cuts))
        factor_of = factor_of * jnp.repeat(jnp.exp(steps), dims[axis_at] // blocks).reshape((-1,) + (1,) * (len(dims) - 1 - axis_at))
    return factor_of


def gaussian(rng, dims, scale, most, split=(), held_as=jnp.bfloat16):
    loudness = block_scale(rng, dims, split, -0.22, 0.18) if split else 1.0
    result = jax.random.normal(rng, dims, jnp.float32) * scale * loudness
    return jnp.minimum(jnp.maximum(result, -most), most).astype(held_as)


def setup_inputs(seed: int = 0) -> dict:
    seeds = jax.random.split(jax.random.key(seed), 9)
    return {
        "features": gaussian(seeds[0], (NODES, F_IN), 1.0, 6.0, ((0, 256),)),
        "block_rows": set_ends(jax.random.randint(seeds[1], (N_ROW, N_COL, NNZ), 0, N_COL * BLK_DEV), jax.random.fold_in(seeds[1], 1), 0, (N_COL * BLK_DEV) - 1).astype(jnp.int32),
        "block_cols": set_ends(jax.random.randint(seeds[2], (N_ROW, N_COL, NNZ), 0, N_ROW * BLK_DEV), jax.random.fold_in(seeds[2], 1), 0, (N_ROW * BLK_DEV) - 1).astype(jnp.int32),
        "block_values": gaussian(seeds[3], (N_ROW, N_COL, NNZ, BS, BS), (NNZ // BLK_DEV * BS) ** -0.5, 0.125, ((0, 8), (1, 32))),
        "weight_one": gaussian(seeds[4], (F_IN, HID), F_IN ** -0.5, 0.5),
        "bias_one": gaussian(seeds[5], (HID,), 0.5, 3.0, (), jnp.float32),
        "weight_two": gaussian(seeds[6], (HID, HID), HID ** -0.5, 0.375),
        "bias_two": gaussian(seeds[7], (HID,), 0.5, 3.0, (), jnp.float32),
    }


def aggregate(node_feats, global_rows, global_cols, values):
    width = node_feats.shape[1]
    blocks = node_feats.reshape(NBLK, BS, width)
    start = jnp.zeros((NBLK, BS, width), jnp.float32)

    def one_cell(carry, items):
        rows_here, cols_here, vals_here = items
        tiles = blocks[cols_here].astype(jnp.float32)
        prod = jnp.einsum("eij,ejf->eif", vals_here.astype(jnp.float32), tiles)
        return carry.at[rows_here].add(prod), None

    total, unused = lax.scan(one_cell, start, (global_rows, global_cols, values))
    return total.reshape(NODES, width).astype(jnp.bfloat16)


def reference(features, block_rows, block_cols, block_values, weight_one, bias_one, weight_two, bias_two):
    row_idx = jnp.arange(N_ROW, dtype=jnp.int32)[:, None, None]
    col_idx = jnp.arange(N_COL, dtype=jnp.int32)[None, :, None]
    global_rows = (row_idx * (N_COL * BLK_DEV) + block_rows).astype(jnp.int32)
    global_cols = (((block_cols // BLK_DEV) * N_COL + col_idx) * BLK_DEV + block_cols % BLK_DEV).astype(jnp.int32)
    cells = N_ROW * N_COL
    global_rows = global_rows.reshape(cells, NNZ)
    global_cols = global_cols.reshape(cells, NNZ)
    values = block_values.reshape(cells, NNZ, BS, BS)
    agg_one = aggregate(features, global_rows, global_cols, values)
    hidden_one = jax.nn.relu(jnp.dot(agg_one, weight_one, preferred_element_type=jnp.float32) + bias_one).astype(jnp.bfloat16)
    agg_two = aggregate(hidden_one, global_rows, global_cols, values)
    return jax.nn.relu(jnp.dot(agg_two, weight_two, preferred_element_type=jnp.float32) + bias_two).astype(jnp.bfloat16)
```

```python
import functools

import jax
import jax.numpy as jnp
from jax import lax
from jax.experimental import pallas as pl
from jax.experimental.pallas import tpu as pltpu
from jax.sharding import PartitionSpec as P

MESH = pl.DeviceIdType.MESH
BF = jnp.bfloat16
F32 = jnp.float32
BS = 128
NNZ = 64
RING = 8
UNITS = 12


def loop(n, body):
    lax.fori_loop(0, n, lambda i, carry: (body(i), carry)[1], 0)


def kernel(
    feat, rows, cols, vals, w1_in, b1_in, w2_in, b2_in, out,
    v, x, a, h, s, agg, w1, b1, w2, b2, rows_v, cols_v, idx_v, idx,
    sib_out, sib_in, q, comb, t1, r1, f, n12, n3, t2, r2,
    rs_send, rs_recv, ag_send, ag_recv, local_sem,
):
    row, col = lax.axis_index("row"), lax.axis_index("col")
    core, cx, cy = lax.rem(col, 2), lax.rem(col // 2, 4), col // 8

    def at(dz=0, dy=0, dx=0, other=False):
        yy, xx = lax.rem(cy + dy + 4, 4), lax.rem(cx + dx + 4, 4)
        kk = 1 - core if other else core
        return (lax.rem(row + dz + RING, RING), (yy * 4 + xx) * 2 + kk)

    up, down, sibling = at(dz=1), at(dz=-1), at(other=True)
    ways = (
        (at(dx=1), at(dx=-1), at(dy=1), at(dy=-1)),
        (at(dy=1), at(dy=-1), at(dx=1), at(dx=-1)),
    )
    barrier = pltpu.get_barrier_semaphore()
    for device in (up, down, sibling) + ways[0]:
        pl.semaphore_signal(barrier, inc=1, device_id=device, device_id_type=MESH)

    loads = []
    for i, (src, dst) in enumerate((
        (rows, rows_v), (cols, cols_v), (feat, x.at[0]), (vals, v), (w1_in, w1), (b1_in, b1), (w2_in, w2), (b2_in, b2),
    )):
        loads.append(pltpu.make_async_copy(src, dst, local_sem.at[i]))
        loads[-1].start()

    loads[0].wait()
    loads[1].wait()
    wide = jnp.broadcast_to(rows_v[...], (NNZ, NNZ))
    sub = lax.broadcasted_iota(jnp.int32, (NNZ, NNZ), 0)
    lane = lax.broadcasted_iota(jnp.int32, (NNZ, NNZ), 1)
    tall = jnp.sum(jnp.where(sub == lane, wide, 0), axis=1, keepdims=True)
    before = jnp.max(jnp.where((tall == wide) & (sub < lane), sub, -1), axis=0, keepdims=True)
    sub = lax.broadcasted_iota(jnp.int32, (NNZ, BS), 0)
    lane = lax.broadcasted_iota(jnp.int32, (NNZ, BS), 1)
    last = jnp.max(jnp.where(tall == lane, sub, -1), axis=0, keepdims=True)
    held = cols_v[...]
    slot = (((held >> 2) - row + RING) & (RING - 1)) * 4 + (held & 3)
    idx_v[...] = jnp.zeros_like(idx_v)
    idx_v[0:1, :] = jnp.where(last < 0, NNZ, last)
    idx_v[1:2, 0:NNZ] = jnp.where(before < 0, NNZ, before)
    idx_v[2:3, 0:NNZ] = slot
    to_scalars = pltpu.make_async_copy(idx_v, idx, local_sem.at[8])
    to_scalars.start()
    s[0, NNZ] = jnp.zeros((BS, BS), F32)
    s[1, NNZ] = jnp.zeros((BS, BS), F32)

    sends = []

    def send(src, dst, sems, at_sem, device):
        copy = pltpu.make_async_remote_copy(
            src_ref=src, dst_ref=dst, send_sem=sems[0].at[at_sem], recv_sem=sems[1].at[at_sem],
            device_id=device, device_id_type=MESH,
        )
        copy.start()
        sends.append(copy)
        return copy

    class Gather:
        def __init__(self, buf, part, number, even):
            self.buf, self.part, self.number = buf, part, number
            self.far = (4, 3) if even else (3, 4)
            self.flying = {}

        def hop(self, n):
            for way, device, source, target in (
                (0, up, (RING - n + 1) % RING, RING - n),
                (1, down, n - 1, n),
            ):
                if n <= self.far[way]:
                    self.flying[way, n] = send(
                        self.buf.at[source, self.part], self.buf.at[target, self.part],
                        (ag_send, ag_recv), (self.number, target - 1), device,
                    )

        def arrive(self, n):
            slots = []
            for way, target in ((0, RING - n), (1, n)):
                if n <= self.far[way]:
                    self.flying[way, n].wait_recv()
                    slots.append(target)
            if n < 4:
                self.hop(n + 1)
            return slots

    loads[2].wait()
    pl.semaphore_wait(barrier, 7)
    first = [Gather(x, pl.ds(2 * j, 2), j, j == 0) for j in range(2)]
    for g in first:
        g.hop(1)
    for n in range(1, 5):
        for g in first:
            g.arrive(n)
    for copy in loads[3:]:
        copy.wait()
    to_scalars.wait()

    def products(half, source):
        def body(i):
            for j in range(8):
                e = i * 8 + j
                held = source(idx[2, e])
                s[half, e] = jnp.dot(v[e], held, preferred_element_type=F32) + s[half, idx[1, e]]

        loop(NNZ // 8, body)

    class Unit:
        def __init__(self, number, half, t):
            self.u, self.half, self.t = number, half, t
            self.kind = t % 2
            self.plus1, self.minus1, self.plus2, self.minus2 = ways[self.kind]

        def send(self, src, dst, which, device):
            return send(src, dst, (rs_send, rs_recv), (self.u, which), device)

        def own(self, d, g, kk):
            if self.kind == 0:
                xx, yy = (cx + d) & 3, (cy + g) & 3
            else:
                yy, xx = (cy + d) & 3, (cx + g) & 3
            b = ((yy * 4 + xx) * 2 + kk) * 4 + self.t
            return s[self.half, idx[0, b]]

        def chip(self, d, g):
            return self.own(d, g, core) + sib_in[self.u, d * 4 + g].astype(F32)

        def stage0(self):
            u = self.u

            def body(i):
                for g in range(4):
                    sib_out[u, i * 4 + g] = self.own(i, g, 1 - core).astype(BF)

            loop(4, body)
            self.sib = self.send(sib_out.at[u], sib_in.at[u], 0, sibling)

        def stage1(self):
            u = self.u
            self.sib.wait_recv()

            def far(g):
                q[u, g] = self.chip(2, g).astype(BF)

            def near(i):
                q[u, 4 + i] = self.chip(1 + 2 * (i // 2), (i + 2) & 3).astype(BF)

            loop(4, far)
            self.m1 = [
                self.send(q.at[u, pl.ds(0, 2)], t1.at[u, pl.ds(0, 2)], 1, self.plus1),
                self.send(q.at[u, pl.ds(2, 2)], t1.at[u, pl.ds(2, 2)], 2, self.minus1),
            ]
            loop(4, near)
            self.m2 = [
                self.send(q.at[u, pl.ds(4, 2)], r1.at[u, 0, pl.ds(2, 2)], 3, self.plus1),
                self.send(q.at[u, pl.ds(6, 2)], r1.at[u, 1, pl.ds(0, 2)], 4, self.minus1),
            ]

        def stage2(self):
            u = self.u
            for copy in self.m1:
                copy.wait_recv()

            def body(i):
                comb[u, i] = (self.chip(1 + 2 * (i // 2), i) + t1[u, i].astype(F32)).astype(BF)

            loop(4, body)
            self.m3 = [
                self.send(comb.at[u, pl.ds(0, 2)], r1.at[u, 0, pl.ds(0, 2)], 5, self.plus1),
                self.send(comb.at[u, pl.ds(2, 2)], r1.at[u, 1, pl.ds(2, 2)], 6, self.minus1),
            ]

        def stage3(self):
            u = self.u
            for copy in self.m2 + self.m3:
                copy.wait_recv()

            def body(g):
                f[u, g] = self.chip(0, g) + (r1[u, 0, g].astype(F32) + r1[u, 1, g].astype(F32))

            loop(4, body)
            n12[u, 0] = f[u, 2, 0:64].astype(BF)
            n12[u, 1] = f[u, 2, 64:128].astype(BF)
            n12[u, 2] = f[u, 1, 64:128].astype(BF)
            n12[u, 3] = f[u, 3, 0:64].astype(BF)
            self.n1 = [
                self.send(n12.at[u, 0], t2.at[u, 0], 7, self.plus2),
                self.send(n12.at[u, 1], t2.at[u, 1], 8, self.minus2),
            ]
            self.n2 = [
                self.send(n12.at[u, 2], r2.at[u, 0, pl.ds(64, 64)], 9, self.plus2),
                self.send(n12.at[u, 3], r2.at[u, 1, pl.ds(0, 64)], 10, self.minus2),
            ]

        def stage4(self):
            u = self.u
            for copy in self.n1:
                copy.wait_recv()
            n3[u, 0] = (f[u, 1, 0:64] + t2[u, 0].astype(F32)).astype(BF)
            n3[u, 1] = (f[u, 3, 64:128] + t2[u, 1].astype(F32)).astype(BF)
            self.n3 = [
                self.send(n3.at[u, 0], r2.at[u, 0, pl.ds(0, 64)], 11, self.plus2),
                self.send(n3.at[u, 1], r2.at[u, 1, pl.ds(64, 64)], 12, self.minus2),
            ]

        def stage5(self):
            u = self.u
            for copy in self.n2 + self.n3:
                copy.wait_recv()
            return (f[u, 0] + (r2[u, 0].astype(F32) + r2[u, 1].astype(F32))).astype(BF)

    def hidden(n, t):
        made = jnp.dot(a[n, t], w1[...], preferred_element_type=F32) + b1[...]
        made = jnp.maximum(made, 0.0).astype(BF)
        h[0, n * 4 + t] = made[:, :BS]
        h[1, n * 4 + t] = made[:, BS:]

    products(0, lambda n: x[n // 4, n % 4])
    units = [Unit(t, 0, t) for t in range(4)]
    pairs = [units[0:2], units[2:4]]
    second = [Gather(a, t, 2 + t, t % 2 == 0) for t in range(4)]

    def each(pair, stage):
        for unit in pair:
            getattr(unit, stage)()

    def publish(pair):
        for unit in pair:
            a[0, unit.t] = unit.stage5()
            second[unit.t].hop(1)
        for unit in pair:
            hidden(0, unit.t)

    def arrive(n, ts):
        slots = [(t, second[t].arrive(n)) for t in ts]
        for t, filled in slots:
            for slot_at in filled:
                hidden(slot_at, t)

    each(pairs[0], "stage0")
    each(pairs[1], "stage0")
    each(pairs[0], "stage1")
    each(pairs[0], "stage2")
    each(pairs[1], "stage1")
    each(pairs[0], "stage3")
    each(pairs[1], "stage2")
    each(pairs[0], "stage4")
    each(pairs[1], "stage3")
    publish(pairs[0])
    each(pairs[1], "stage4")
    arrive(1, (0, 1))
    publish(pairs[1])
    arrive(2, (0, 1))
    arrive(1, (2, 3))
    arrive(3, (0, 1))
    arrive(2, (2, 3))
    arrive(4, (0, 1))
    arrive(3, (2, 3))
    arrive(4, (2, 3))

    units = [Unit(4 + i, i // 4, i % 4) for i in range(8)]
    pairs = [units[2 * i : 2 * i + 2] for i in range(4)]

    def finish(pair):
        for unit in pair:
            agg[unit.t, :, unit.half * BS : (unit.half + 1) * BS] = unit.stage5()

    products(0, lambda n: h[0, n])
    each(pairs[0], "stage0")
    each(pairs[1], "stage0")
    each(pairs[0], "stage1")
    each(pairs[1], "stage1")
    products(1, lambda n: h[1, n])
    each(pairs[0], "stage2")
    each(pairs[2], "stage0")
    each(pairs[1], "stage2")
    each(pairs[2], "stage1")
    each(pairs[0], "stage3")
    each(pairs[3], "stage0")
    each(pairs[2], "stage2")
    each(pairs[3], "stage1")
    each(pairs[1], "stage3")
    each(pairs[0], "stage4")
    each(pairs[3], "stage2")
    each(pairs[2], "stage3")
    each(pairs[1], "stage4")
    finish(pairs[0])
    each(pairs[3], "stage3")
    each(pairs[2], "stage4")
    finish(pairs[1])
    each(pairs[3], "stage4")
    finish(pairs[2])
    finish(pairs[3])
    for t in range(4):
        made = jnp.dot(agg[t], w2[...], preferred_element_type=F32) + b2[...]
        out[t * BS : (t + 1) * BS, :] = jnp.maximum(made, 0.0).astype(BF)
    for copy in sends:
        copy.wait_send()


def local(features, block_rows, block_cols, block_values, weight_one, bias_one, weight_two, bias_two):
    block = (BS, BS)
    return pl.pallas_call(
        kernel,
        out_shape=jax.ShapeDtypeStruct((512, 256), BF),
        in_specs=[pl.BlockSpec(memory_space=pl.ANY)] * 8,
        out_specs=pl.BlockSpec(memory_space=pltpu.VMEM),
        scratch_shapes=[
            pltpu.VMEM((NNZ, *block), BF),
            pltpu.VMEM((RING, 4, *block), BF),
            pltpu.VMEM((RING, 4, *block), BF),
            pltpu.VMEM((2, RING * 4, *block), BF),
            pltpu.VMEM((2, NNZ + 1, *block), F32),
            pltpu.VMEM((4, BS, 2 * BS), BF),
            pltpu.VMEM((128, 256), BF),
            pltpu.VMEM((1, 256), F32),
            pltpu.VMEM((256, 256), BF),
            pltpu.VMEM((1, 256), F32),
            pltpu.VMEM((1, NNZ), jnp.int32),
            pltpu.VMEM((1, NNZ), jnp.int32),
            pltpu.VMEM((8, BS), jnp.int32),
            pltpu.SMEM((8, BS), jnp.int32),
            pltpu.VMEM((UNITS, 16, *block), BF),
            pltpu.VMEM((UNITS, 16, *block), BF),
            pltpu.VMEM((UNITS, 8, *block), BF),
            pltpu.VMEM((UNITS, 4, *block), BF),
            pltpu.VMEM((UNITS, 4, *block), BF),
            pltpu.VMEM((UNITS, 2, 4, *block), BF),
            pltpu.VMEM((UNITS, 4, *block), F32),
            pltpu.VMEM((UNITS, 4, 64, BS), BF),
            pltpu.VMEM((UNITS, 2, 64, BS), BF),
            pltpu.VMEM((UNITS, 2, 64, BS), BF),
            pltpu.VMEM((UNITS, 2, *block), BF),
            pltpu.SemaphoreType.DMA((UNITS, 13)),
            pltpu.SemaphoreType.DMA((UNITS, 13)),
            pltpu.SemaphoreType.DMA((6, 7)),
            pltpu.SemaphoreType.DMA((6, 7)),
            pltpu.SemaphoreType.DMA((9,)),
        ],
        compiler_params=pltpu.CompilerParams(
            collective_id=1, has_side_effects=True, vmem_limit_bytes=56 * 2**20
        ),
        name="two_layers",
    )(
        features.reshape(4, *block),
        block_rows.reshape(1, NNZ),
        block_cols.reshape(1, NNZ),
        block_values.reshape(NNZ, *block),
        weight_one,
        bias_one.reshape(1, -1),
        weight_two,
        bias_two.reshape(1, -1),
    )


def solution(mesh):
    placed = (
        P(("row", "col"), None),
        P("row", "col", None),
        P("row", "col", None),
        P("row", "col", None, None, None),
        P(),
        P(),
        P(),
        P(),
    )
    return jax.shard_map(
        local, mesh=mesh, in_specs=placed, out_specs=P(("row", "col"), None), check_vma=False
    )
```

```python
import functools

import jax
import jax.numpy as jnp
from jax import lax
from jax.experimental import pallas as pl
from jax.experimental.pallas import tpu as pltpu
from jax.sharding import PartitionSpec as P

MESH = pl.DeviceIdType.MESH
BF = jnp.bfloat16
F32 = jnp.float32
BS = 128
NNZ = 64
RING = 8
UNITS = 12


def loop(n, body):
    lax.fori_loop(0, n, lambda i, carry: (body(i), carry)[1], 0)


def kernel(
    feat, rows, cols, vals, w1_in, b1_in, w2_in, b2_in, out,
    v, x, a, h, s, agg, w1, b1, w2, b2, rows_v, cols_v, idx_v, idx,
    sib_out, sib_in, q, comb, t1, r1, f, fb, r2, out_v,
    rs_send, rs_recv, ag_send, ag_recv, local_sem, out_sem,
):
    row, col = lax.axis_index("row"), lax.axis_index("col")
    core, cx, cy = lax.rem(col, 2), lax.rem(col // 2, 4), col // 8

    def at(dz=0, dy=0, dx=0, other=False):
        yy, xx = lax.rem(cy + dy + 4, 4), lax.rem(cx + dx + 4, 4)
        kk = 1 - core if other else core
        return (lax.rem(row + dz + RING, RING), (yy * 4 + xx) * 2 + kk)

    sibling = at(other=True)
    along_z = {step: at(dz=step) for step in (1, -1, 2, -2)}
    along_x = {step: at(dx=step) for step in (1, 2, -1)}
    along_y = {step: at(dy=step) for step in (1, 2, -1)}
    ways = ((along_x, along_y), (along_y, along_x))
    barrier = pltpu.get_barrier_semaphore()
    peers = [sibling, *along_z.values(), *along_x.values(), *along_y.values()]
    for device in peers:
        pl.semaphore_signal(barrier, inc=1, device_id=device, device_id_type=MESH)

    loads = []
    for i, (src, dst) in enumerate((
        (feat, x.at[0]), (rows, rows_v), (cols, cols_v), (vals, v), (w1_in, w1), (b1_in, b1), (w2_in, w2), (b2_in, b2),
    )):
        loads.append(pltpu.make_async_copy(src, dst, local_sem.at[i]))
        loads[-1].start()

    sends = []

    def send(src, dst, sems, at_sem, device):
        copy = pltpu.make_async_remote_copy(
            src_ref=src, dst_ref=dst, send_sem=sems[0].at[at_sem], recv_sem=sems[1].at[at_sem],
            device_id=device, device_id_type=MESH,
        )
        copy.start()
        sends.append(copy)
        return copy

    class Gather:
        def __init__(self, buf, part, number, plan):
            self.buf, self.part, self.number, self.plan = buf, part, number, plan
            self.flying = {}

        def start(self, n, source):
            for slot_at, step in self.plan[n]:
                if slot_at == source:
                    target = (slot_at - step) % RING
                    self.flying[target] = send(
                        self.buf.at[slot_at, self.part], self.buf.at[target, self.part],
                        (ag_send, ag_recv), (self.number, target - 1), along_z[step],
                    )

        def arrive(self, n):
            filled = [(slot_at - step) % RING for slot_at, step in self.plan[n]]
            for target in filled:
                self.flying[target].wait_recv()
                if n + 1 < len(self.plan):
                    self.start(n + 1, target)
            return filled

    ring = (
        (((0, 1), (0, -1)), ((7, 1), (1, -1)), ((6, 1), (2, -1)), ((5, 1),)),
        (((0, 1), (0, -1)), ((7, 1), (1, -1)), ((6, 1), (2, -1)), ((3, -1),)),
    )
    three = (
        (((0, 1), (0, -1)), ((7, 1), (1, -1)), ((6, 2), (6, 1), (2, -1))),
        (((0, 1), (0, -1)), ((7, 1), (1, -1)), ((2, -2), (6, 1), (2, -1))),
    )
    two = (
        (((0, 2), (0, -2), (0, 1), (0, -1)), ((6, 2), (6, 1), (2, -1))),
        (((0, 2), (0, -2), (0, 1), (0, -1)), ((2, -2), (6, 1), (2, -1))),
    )

    loads[0].wait()
    pl.semaphore_wait(barrier, len(peers))
    first = [Gather(x, t, t, three[t % 2]) for t in range(4)]
    for g in first:
        g.start(0, 0)
    loads[1].wait()
    loads[2].wait()
    wide = jnp.broadcast_to(rows_v[...], (NNZ, NNZ))
    sub = lax.broadcasted_iota(jnp.int32, (NNZ, NNZ), 0)
    lane = lax.broadcasted_iota(jnp.int32, (NNZ, NNZ), 1)
    tall = jnp.sum(jnp.where(sub == lane, wide, 0), axis=1, keepdims=True)
    before = jnp.max(jnp.where((tall == wide) & (sub < lane), sub, -1), axis=0, keepdims=True)
    sub = lax.broadcasted_iota(jnp.int32, (NNZ, BS), 0)
    lane = lax.broadcasted_iota(jnp.int32, (NNZ, BS), 1)
    last = jnp.max(jnp.where(tall == lane, sub, -1), axis=0, keepdims=True)
    held = cols_v[...]
    slot = (((held >> 2) - row + RING) & (RING - 1)) * 4 + (held & 3)
    idx_v[...] = jnp.zeros_like(idx_v)
    idx_v[0:1, :] = jnp.where(last < 0, NNZ, last)
    idx_v[1:2, 0:NNZ] = jnp.where(before < 0, NNZ, before)
    idx_v[2:3, 0:NNZ] = slot
    to_scalars = pltpu.make_async_copy(idx_v, idx, local_sem.at[8])
    to_scalars.start()
    s[0, NNZ] = jnp.zeros((BS, BS), F32)
    s[1, NNZ] = jnp.zeros((BS, BS), F32)

    for n in range(len(three[0])):
        for g in first:
            g.arrive(n)
    for copy in loads[3:]:
        copy.wait()
    to_scalars.wait()

    def products(half, source):
        def body(i):
            for j in range(8):
                e = i * 8 + j
                held = source(idx[2, e])
                s[half, e] = jnp.dot(v[e], held, preferred_element_type=F32) + s[half, idx[1, e]]

        loop(NNZ // 8, body)

    class Unit:
        def __init__(self, number, half, t):
            self.u, self.half, self.t = number, half, t
            self.kind = t % 2
            self.way1, self.way2 = ways[self.kind]

        def send(self, src, dst, which, device):
            return send(src, dst, (rs_send, rs_recv), (self.u, which), device)

        def own(self, d, g, kk):
            if self.kind == 0:
                xx, yy = (cx + d) & 3, (cy + g) & 3
            else:
                yy, xx = (cy + d) & 3, (cx + g) & 3
            b = ((yy * 4 + xx) * 2 + kk) * 4 + self.t
            return s[self.half, idx[0, b]]

        def chip(self, d, e, g):
            return self.own(d, g, core) + sib_in[self.u, e * 4 + g].astype(F32)

        def stage0(self):
            u = self.u
            self.sib = []
            for which, at_e, d, step, n in ((0, 0, 2, 0, 1), (1, 1, 1, 2, 2), (2, 3, 0, 0, 1)):

                def body(i):
                    for g in range(4):
                        sib_out[u, at_e * 4 + i * 4 + g] = self.own(d + step * i, g, 1 - core).astype(BF)

                loop(n, body)
                part = pl.ds(at_e * 4, n * 4)
                self.sib.append(self.send(sib_out.at[u, part], sib_in.at[u, part], which, sibling))

        def far(self):
            u = self.u
            self.sib[0].wait_recv()

            def body(g):
                q[u, g] = self.chip(2, 0, g).astype(BF)

            loop(4, body)
            self.m1 = [
                self.send(q.at[u, pl.ds(0, 2)], t1.at[u, pl.ds(0, 2)], 3, self.way1[1]),
                self.send(q.at[u, pl.ds(2, 2)], t1.at[u, pl.ds(2, 2)], 4, self.way1[-1]),
            ]

        def near(self):
            u = self.u
            self.sib[1].wait_recv()

            def body(i):
                q[u, 4 + i] = self.chip(1 + 2 * (i // 2), 1 + i // 2, (i + 2) & 3).astype(BF)

            loop(4, body)
            self.m2 = [
                self.send(q.at[u, pl.ds(4, 2)], r1.at[u, 0, pl.ds(2, 2)], 5, self.way1[1]),
                self.send(q.at[u, pl.ds(6, 2)], r1.at[u, 1, pl.ds(0, 2)], 6, self.way1[-1]),
            ]

        def passed(self):
            u = self.u
            for copy in self.m1:
                copy.wait_recv()

            def body(i):
                held = self.chip(1 + 2 * (i // 2), 1 + i // 2, i)
                comb[u, i] = (held + t1[u, i].astype(F32)).astype(BF)

            loop(4, body)
            self.m3 = [
                self.send(comb.at[u, pl.ds(0, 2)], r1.at[u, 0, pl.ds(0, 2)], 7, self.way1[1]),
                self.send(comb.at[u, pl.ds(2, 2)], r1.at[u, 1, pl.ds(2, 2)], 8, self.way1[-1]),
            ]

        def second(self):
            u = self.u
            self.sib[2].wait_recv()
            for copy in self.m2 + self.m3:
                copy.wait_recv()
            self.n = []
            for g in (2, 1, 3, 0):
                held = self.chip(0, 3, g) + (r1[u, 0, g].astype(F32) + r1[u, 1, g].astype(F32))
                if g == 0:
                    f[u] = held
                else:
                    fb[u, g - 1] = held.astype(BF)
                    step = -1 if g == 3 else g
                    self.n.append(self.send(fb.at[u, g - 1], r2.at[u, g - 1], 8 + g, self.way2[step]))

        def total(self):
            u = self.u
            for copy in self.n:
                copy.wait_recv()
            return (f[u] + r2[u, 0].astype(F32) + (r2[u, 1].astype(F32) + r2[u, 2].astype(F32))).astype(BF)

    def hidden(n, t):
        made = jnp.dot(a[n, t], w1[...], preferred_element_type=F32) + b1[...]
        made = jnp.maximum(made, 0.0).astype(BF)
        h[0, n * 4 + t] = made[:, :BS]
        h[1, n * 4 + t] = made[:, BS:]

    products(0, lambda n: x[n // 4, n % 4])
    units = [Unit(t, 0, t) for t in range(4)]
    pairs = [units[0:2], units[2:4]]
    second = [Gather(a, t, 4 + t, (three, three)[t // 2][t % 2]) for t in range(4)]

    def each(pair, stage):
        for unit in pair:
            getattr(unit, stage)()

    def publish(pair):
        for unit in pair:
            a[0, unit.t] = unit.total()
            second[unit.t].start(0, 0)
        for unit in pair:
            hidden(0, unit.t)

    def arrive(n, ts):
        slots = [(t, second[t].arrive(n)) for t in ts if n < len(second[t].plan)]
        for t, filled in slots:
            for slot_at in filled:
                hidden(slot_at, t)

    each(units, "stage0")
    each(units, "far")
    each(pairs[0], "near")
    each(pairs[0], "passed")
    each(pairs[1], "near")
    each(pairs[1], "passed")
    each(pairs[0], "second")
    each(pairs[1], "second")
    publish(pairs[0])
    publish(pairs[1])
    for n in range(4):
        arrive(n, (0, 1))
        arrive(n, (2, 3))

    units = [Unit(4 + i, i // 4, i % 4) for i in range(8)]
    pairs = [units[2 * i : 2 * i + 2] for i in range(4)]

    def finish(pair):
        for unit in pair:
            agg[unit.t, :, unit.half * BS : (unit.half + 1) * BS] = unit.total()

    products(0, lambda n: h[0, n])
    each(pairs[0] + pairs[1], "stage0")
    each(pairs[0], "far")
    each(pairs[1], "far")
    each(pairs[0], "near")
    products(1, lambda n: h[1, n])
    each(pairs[2] + pairs[3], "stage0")
    each(pairs[0], "passed")
    each(pairs[1], "near")
    each(pairs[2], "far")
    each(pairs[1], "passed")
    each(pairs[0], "second")
    each(pairs[2], "near")
    each(pairs[3], "far")
    each(pairs[2], "passed")
    each(pairs[1], "second")
    each(pairs[3], "near")
    each(pairs[3], "passed")
    finish(pairs[0])
    each(pairs[2], "second")
    finish(pairs[1])
    each(pairs[3], "second")
    written = []

    def put(t):
        made = jnp.dot(agg[t], w2[...], preferred_element_type=F32) + b2[...]
        out_v[t] = jnp.maximum(made, 0.0).astype(BF)
        written.append(pltpu.make_async_copy(out_v.at[t], out.at[t], out_sem.at[t]))
        written[-1].start()

    finish(pairs[2])
    put(0)
    put(1)
    finish(pairs[3])
    put(2)
    put(3)
    for copy in sends:
        copy.wait_send()
    for copy in written:
        copy.wait()


def local(features, block_rows, block_cols, block_values, weight_one, bias_one, weight_two, bias_two):
    block = (BS, BS)
    return pl.pallas_call(
        kernel,
        out_shape=jax.ShapeDtypeStruct((4, BS, 2 * BS), BF),
        in_specs=[pl.BlockSpec(memory_space=pl.ANY)] * 8,
        out_specs=pl.BlockSpec(memory_space=pl.ANY),
        scratch_shapes=[
            pltpu.VMEM((NNZ, *block), BF),
            pltpu.VMEM((RING, 4, *block), BF),
            pltpu.VMEM((RING, 4, *block), BF),
            pltpu.VMEM((2, RING * 4, *block), BF),
            pltpu.VMEM((2, NNZ + 1, *block), F32),
            pltpu.VMEM((4, BS, 2 * BS), BF),
            pltpu.VMEM((128, 256), BF),
            pltpu.VMEM((1, 256), F32),
            pltpu.VMEM((256, 256), BF),
            pltpu.VMEM((1, 256), F32),
            pltpu.VMEM((1, NNZ), jnp.int32),
            pltpu.VMEM((1, NNZ), jnp.int32),
            pltpu.VMEM((8, BS), jnp.int32),
            pltpu.SMEM((8, BS), jnp.int32),
            pltpu.VMEM((UNITS, 16, *block), BF),
            pltpu.VMEM((UNITS, 16, *block), BF),
            pltpu.VMEM((UNITS, 8, *block), BF),
            pltpu.VMEM((UNITS, 4, *block), BF),
            pltpu.VMEM((UNITS, 4, *block), BF),
            pltpu.VMEM((UNITS, 2, 4, *block), BF),
            pltpu.VMEM((UNITS, *block), F32),
            pltpu.VMEM((UNITS, 3, *block), BF),
            pltpu.VMEM((UNITS, 3, *block), BF),
            pltpu.VMEM((4, BS, 2 * BS), BF),
            pltpu.SemaphoreType.DMA((UNITS, 12)),
            pltpu.SemaphoreType.DMA((UNITS, 12)),
            pltpu.SemaphoreType.DMA((8, 7)),
            pltpu.SemaphoreType.DMA((8, 7)),
            pltpu.SemaphoreType.DMA((9,)),
            pltpu.SemaphoreType.DMA((4,)),
        ],
        compiler_params=pltpu.CompilerParams(
            collective_id=1, has_side_effects=True, vmem_limit_bytes=56 * 2**20
        ),
        name="two_layers",
    )(
        features.reshape(4, *block),
        block_rows.reshape(1, NNZ),
        block_cols.reshape(1, NNZ),
        block_values.reshape(NNZ, *block),
        weight_one,
        bias_one.reshape(1, -1),
        weight_two,
        bias_two.reshape(1, -1),
    ).reshape(512, 256)


def solution(mesh):
    placed = (
        P(("row", "col"), None),
        P("row", "col", None),
        P("row", "col", None),
        P("row", "col", None, None, None),
        P(),
        P(),
        P(),
        P(),
    )
    return jax.shard_map(
        local, mesh=mesh, in_specs=placed, out_specs=P(("row", "col"), None), check_vma=False
    )
```

```python
import functools

import jax
import jax.numpy as jnp
from jax import lax
from jax.experimental import pallas as pl
from jax.experimental.pallas import tpu as pltpu
from jax.sharding import PartitionSpec as P

MESH = pl.DeviceIdType.MESH
BF = jnp.bfloat16
F32 = jnp.float32
BS = 128
NNZ = 64
RING = 8
PAIRS = 6
SIB, FIRST, COMB, SECOND, GATHER1, GATHER2 = range(6)
SIB_FAR, SIB_NEAR, FAR, SUMS, LAST_SUMS, TOTAL = range(6)


def loop(n, body):
    lax.fori_loop(0, n, lambda i, carry: (body(i), carry)[1], 0)


def kernel(
    feat, rows, cols, vals, w1_in, b1_in, w2_in, b2_in, out,
    v, x, a, h, s, agg, w1, b1, w2, b2, rows_v, cols_v, idx_v, idx,
    sib_out, sib_in, q, comb, t1, r1, f, fb, r2,
    sent, rs_recv, ag_recv, local_sem,
):
    row, col = lax.axis_index("row"), lax.axis_index("col")
    core, cx, cy = lax.rem(col, 2), lax.rem(col // 2, 4), col // 8

    def at(dz=0, dy=0, dx=0, other=False):
        yy, xx = lax.rem(cy + dy + 4, 4), lax.rem(cx + dx + 4, 4)
        kk = 1 - core if other else core
        return (lax.rem(row + dz + RING, RING), (yy * 4 + xx) * 2 + kk)

    sibling = at(other=True)
    along_z = {step: at(dz=step) for step in (1, -1, 2, -2)}
    along_x = {step: at(dx=step) for step in (1, 2, -1)}
    along_y = {step: at(dy=step) for step in (1, 2, -1)}
    ways = ((along_x, along_y), (along_y, along_x))
    barrier = pltpu.get_barrier_semaphore()
    peers = [sibling, *along_z.values(), *along_x.values(), *along_y.values()]
    for device in peers:
        pl.semaphore_signal(barrier, inc=1, device_id=device, device_id_type=MESH)

    loads = []
    for i, (src, dst) in enumerate((
        (feat, x.at[0]), (rows, rows_v), (cols, cols_v), (vals, v), (w1_in, w1), (b1_in, b1), (w2_in, w2), (b2_in, b2),
    )):
        loads.append(pltpu.make_async_copy(src, dst, local_sem.at[i]))
        loads[-1].start()

    def send(src, dst, kind, recv_sem, device):
        pltpu.make_async_remote_copy(
            src_ref=src, dst_ref=dst, send_sem=sent.at[kind], recv_sem=recv_sem,
            device_id=device, device_id_type=MESH,
        ).start()

    def arrived(ref, recv_sem):
        pltpu.make_async_remote_copy(
            src_ref=ref, dst_ref=ref, send_sem=sent.at[SIB], recv_sem=recv_sem,
            device_id=sibling, device_id_type=MESH,
        ).wait_recv()

    def all_sent(ref, kind):
        pltpu.make_async_remote_copy(
            src_ref=ref, dst_ref=ref, send_sem=sent.at[kind], recv_sem=rs_recv.at[0, 0],
            device_id=sibling, device_id_type=MESH,
        ).wait_send()

    def rounds(t):
        return (
            ((0, 1), (0, -1)),
            ((7, 1), (1, -1)),
            ((6, 2), (6, 1), (2, -1)) if t % 2 == 0 else ((2, -2), (2, -1), (6, 1)),
        )

    class Gather:
        def __init__(self, buf, layer, t):
            self.buf, self.kind, self.t, self.sems = buf, GATHER1 + layer, t, ag_recv.at[layer * 4 + t]

        def start(self, n, source):
            for slot_at, step in rounds(self.t)[n]:
                if slot_at == source:
                    target = (slot_at - step) % RING
                    send(self.buf.at[slot_at, self.t], self.buf.at[target, self.t], self.kind, self.sems.at[target - 1], along_z[step])

        def arrive(self, n):
            filled = [(slot_at - step) % RING for slot_at, step in rounds(self.t)[n]]
            if n == 2:
                filled.sort(key=lambda target: target == 4)
            for target in filled:
                arrived(self.buf.at[target, self.t], self.sems.at[target - 1])
                if n < 2:
                    self.start(n + 1, target)
            return filled

    loads[0].wait()
    pl.semaphore_wait(barrier, len(peers))
    first = [Gather(x, 0, t) for t in range(4)]
    for g in first:
        g.start(0, 0)
    loads[1].wait()
    loads[2].wait()
    wide = jnp.broadcast_to(rows_v[...], (NNZ, NNZ))
    sub = lax.broadcasted_iota(jnp.int32, (NNZ, NNZ), 0)
    lane = lax.broadcasted_iota(jnp.int32, (NNZ, NNZ), 1)
    tall = jnp.sum(jnp.where(sub == lane, wide, 0), axis=1, keepdims=True)
    before = jnp.max(jnp.where((tall == wide) & (sub < lane), sub, -1), axis=0, keepdims=True)
    sub = lax.broadcasted_iota(jnp.int32, (NNZ, BS), 0)
    lane = lax.broadcasted_iota(jnp.int32, (NNZ, BS), 1)
    last = jnp.max(jnp.where(tall == lane, sub, -1), axis=0, keepdims=True)
    held = cols_v[...]
    slot = (((held >> 2) - row + RING) & (RING - 1)) * 4 + (held & 3)
    idx_v[...] = jnp.zeros_like(idx_v)
    idx_v[0:1, :] = jnp.where(last < 0, NNZ, last)
    idx_v[1:2, 0:NNZ] = jnp.where(before < 0, NNZ, before)
    idx_v[2:3, 0:NNZ] = slot
    to_scalars = pltpu.make_async_copy(idx_v, idx, local_sem.at[8])
    to_scalars.start()
    s[0, NNZ] = jnp.zeros((BS, BS), F32)
    s[1, NNZ] = jnp.zeros((BS, BS), F32)

    for n in range(3):
        for g in first:
            g.arrive(n)
    for copy in loads[3:]:
        copy.wait()
    to_scalars.wait()

    def products(half, source):
        for e in range(NNZ):
            held = source(idx[2, e])
            s[half, e] = jnp.dot(v[e], held, preferred_element_type=F32) + s[half, idx[1, e]]

    class Pair:
        def __init__(self, number, half, j):
            self.p, self.half, self.j, self.sems = number, half, j, rs_recv.at[number]

        def own(self, w, d, g, kk):
            if w == 0:
                xx, yy = (cx + d) & 3, (cy + g) & 3
            else:
                yy, xx = (cy + d) & 3, (cx + g) & 3
            b = ((yy * 4 + xx) * 2 + kk) * 4 + self.j * 2 + w
            return s[self.half, idx[0, b]]

        def chip(self, w, d, e, g):
            return self.own(w, d, g, core) + sib_in[self.p, e, w, g].astype(F32)

        def to_sibling(self, e, d, step, n, sem):
            p = self.p
            for w in range(2):

                def body(i):
                    for g in range(4):
                        sib_out[p, e + i, w, g] = self.own(w, d + step * i, g, 1 - core).astype(BF)

                loop(n, body)
            part = pl.ds(e, n)
            send(sib_out.at[p, part], sib_in.at[p, part], SIB, self.sems.at[sem], sibling)

        def sib_far(self):
            self.to_sibling(0, 2, 0, 1, SIB_FAR)

        def sib_near(self):
            self.to_sibling(1, 1, 2, 2, SIB_NEAR)

        def sib_here(self):
            self.to_sibling(3, 0, 0, 1, SUMS)

        def far(self):
            p = self.p
            arrived(sib_in.at[p, 0], self.sems.at[SIB_FAR])
            for w in range(2):

                def body(g):
                    q[p, w, g] = self.chip(w, 2, 0, g).astype(BF)

                loop(4, body)
                for at_q, step in ((0, 1), (2, -1)):
                    part = pl.ds(at_q, 2)
                    send(q.at[p, w, part], t1.at[p, w, part], FIRST, self.sems.at[FAR], ways[w][0][step])

        def near(self):
            p = self.p
            arrived(sib_in.at[p, pl.ds(1, 2)], self.sems.at[SIB_NEAR])
            for w in range(2):

                def body(i):
                    q[p, w, 4 + i] = self.chip(w, 1 + 2 * (i // 2), 1 + i // 2, (i + 2) & 3).astype(BF)

                loop(4, body)
                for side, step in ((0, 1), (1, -1)):
                    send(
                        q.at[p, w, pl.ds(4 + 2 * side, 2)], r1.at[p, w, side, pl.ds(2 - 2 * side, 2)],
                        FIRST, self.sems.at[SUMS], ways[w][0][step],
                    )

        def passed(self):
            p = self.p
            arrived(t1.at[p], self.sems.at[FAR])
            for n, sem in ((0, SUMS), (1, LAST_SUMS)):
                for w in range(2):
                    for side, step in ((0, 1), (1, -1)):
                        g = 2 * side + n
                        held = self.chip(w, 1 + 2 * side, 1 + side, g)
                        comb[p, w, g] = (held + t1[p, w, g].astype(F32)).astype(BF)
                        send(comb.at[p, w, g], r1.at[p, w, side, g], COMB, self.sems.at[sem], ways[w][0][step])

        def sums(self, w, g):
            p = self.p
            return self.chip(w, 0, 3, g) + (r1[p, w, 0, g].astype(F32) + r1[p, w, 1, g].astype(F32))

        def away(self, w, g):
            p = self.p
            fb[p, w, g - 1] = self.sums(w, g).astype(BF)
            send(fb.at[p, w, g - 1], r2.at[p, w, g - 1], SECOND, self.sems.at[TOTAL], ways[w][1][-1 if g == 3 else g])

        def second(self):
            p = self.p
            arrived(sib_in.at[pl.ds(0, 5), 0, 0], self.sems.at[SUMS])
            for w in range(2):
                self.away(w, 2)
            arrived(r1.at[p, 0, 0], self.sems.at[LAST_SUMS])
            for g in (1, 3):
                for w in range(2):
                    self.away(w, g)
            for w in range(2):
                f[p, w] = self.sums(w, 0)

        def total(self):
            p = self.p
            arrived(r2.at[p], self.sems.at[TOTAL])
            return [
                (f[p, w] + r2[p, w, 0].astype(F32) + (r2[p, w, 1].astype(F32) + r2[p, w, 2].astype(F32))).astype(BF)
                for w in range(2)
            ]

    def hidden(n, t):
        made = jnp.dot(a[n, t], w1[...], preferred_element_type=F32) + b1[...]
        made = jnp.maximum(made, 0.0).astype(BF)
        h[0, n * 4 + t] = made[:, :BS]
        h[1, n * 4 + t] = made[:, BS:]

    products(0, lambda n: x[n // 4, n % 4])
    pairs = [Pair(j, 0, j) for j in range(2)]
    gathers = [Gather(a, 1, t) for t in range(4)]

    def publish(j):
        for w, block in enumerate(pairs[j].total()):
            a[0, 2 * j + w] = block
            gathers[2 * j + w].start(0, 0)
        for w in range(2):
            hidden(0, 2 * j + w)

    def arrive(n, j):
        filled = [(t, slot_at) for t in (2 * j, 2 * j + 1) for slot_at in gathers[t].arrive(n)]
        for t, slot_at in filled:
            hidden(slot_at, t)

    one, two = pairs
    one.sib_far()
    two.sib_far()
    one.sib_near()
    two.sib_near()
    one.sib_here()
    two.sib_here()
    one.far()
    two.far()
    one.near()
    one.passed()
    two.near()
    two.passed()
    one.second()
    two.second()
    publish(0)
    publish(1)
    for n in range(3):
        arrive(n, 0)
        arrive(n, 1)

    pairs = [Pair(2 + i, i // 2, i % 2) for i in range(4)]

    def finish(pair):
        for w, block in enumerate(pair.total()):
            agg[2 * pair.j + w, :, pair.half * BS : (pair.half + 1) * BS] = block

    one, two, three, four = pairs
    products(0, lambda n: h[0, n])
    one.sib_far()
    two.sib_far()
    one.sib_near()
    two.sib_near()
    one.sib_here()
    two.sib_here()
    one.far()
    two.far()
    one.near()
    products(1, lambda n: h[1, n])
    three.sib_far()
    four.sib_far()
    three.sib_near()
    four.sib_near()
    three.sib_here()
    four.sib_here()
    one.passed()
    two.near()
    three.far()
    two.passed()
    three.near()
    four.far()
    three.passed()
    four.near()
    four.passed()
    one.second()
    two.second()
    three.second()
    finish(one)
    finish(two)
    four.second()

    def put(t):
        made = jnp.dot(agg[t], w2[...], preferred_element_type=F32) + b2[...]
        out[t] = jnp.maximum(made, 0.0).astype(BF)

    finish(three)
    put(0)
    put(1)
    finish(four)
    put(2)
    put(3)
    all_sent(sib_out, SIB)
    all_sent(q, FIRST)
    all_sent(comb, COMB)
    all_sent(fb, SECOND)
    all_sent(x.at[pl.ds(1, 7)], GATHER1)
    all_sent(a.at[pl.ds(1, 7)], GATHER2)


def local(features, block_rows, block_cols, block_values, weight_one, bias_one, weight_two, bias_two):
    block = (BS, BS)
    return pl.pallas_call(
        kernel,
        out_shape=pltpu.VMEM((4, BS, 2 * BS), BF),
        in_specs=[pl.BlockSpec(memory_space=pl.ANY)] * 8,
        out_specs=pl.BlockSpec(memory_space=pltpu.VMEM),
        scratch_shapes=[
            pltpu.VMEM((NNZ, *block), BF),
            pltpu.VMEM((RING, 4, *block), BF),
            pltpu.VMEM((RING, 4, *block), BF),
            pltpu.VMEM((2, RING * 4, *block), BF),
            pltpu.VMEM((2, NNZ + 1, *block), F32),
            pltpu.VMEM((4, BS, 2 * BS), BF),
            pltpu.VMEM((128, 256), BF),
            pltpu.VMEM((1, 256), F32),
            pltpu.VMEM((256, 256), BF),
            pltpu.VMEM((1, 256), F32),
            pltpu.VMEM((1, NNZ), jnp.int32),
            pltpu.VMEM((1, NNZ), jnp.int32),
            pltpu.VMEM((8, BS), jnp.int32),
            pltpu.SMEM((8, BS), jnp.int32),
            pltpu.VMEM((PAIRS, 4, 2, 4, *block), BF),
            pltpu.VMEM((PAIRS, 4, 2, 4, *block), BF),
            pltpu.VMEM((PAIRS, 2, 8, *block), BF),
            pltpu.VMEM((PAIRS, 2, 4, *block), BF),
            pltpu.VMEM((PAIRS, 2, 4, *block), BF),
            pltpu.VMEM((PAIRS, 2, 2, 4, *block), BF),
            pltpu.VMEM((PAIRS, 2, *block), F32),
            pltpu.VMEM((PAIRS, 2, 3, *block), BF),
            pltpu.VMEM((PAIRS, 2, 3, *block), BF),
            pltpu.SemaphoreType.DMA((6,)),
            pltpu.SemaphoreType.DMA((PAIRS, 6)),
            pltpu.SemaphoreType.DMA((8, 7)),
            pltpu.SemaphoreType.DMA((9,)),
        ],
        compiler_params=pltpu.CompilerParams(
            collective_id=1, has_side_effects=True, vmem_limit_bytes=56 * 2**20
        ),
        name="two_layers",
    )(
        features.reshape(4, *block),
        block_rows.reshape(1, NNZ),
        block_cols.reshape(1, NNZ),
        block_values.reshape(NNZ, *block),
        weight_one,
        bias_one.reshape(1, -1),
        weight_two,
        bias_two.reshape(1, -1),
    ).reshape(512, 256)


def solution(mesh):
    placed = (
        P(("row", "col"), None),
        P("row", "col", None),
        P("row", "col", None),
        P("row", "col", None, None, None),
        P(),
        P(),
        P(),
        P(),
    )
    return jax.shard_map(
        local, mesh=mesh, in_specs=placed, out_specs=P(("row", "col"), None), check_vma=False
    )
```

```python
import functools

import jax
import jax.numpy as jnp
from jax import lax
from jax.experimental import pallas as pl
from jax.experimental.pallas import tpu as pltpu
from jax.sharding import PartitionSpec as P

MESH = pl.DeviceIdType.MESH
BF = jnp.bfloat16
F32 = jnp.float32
BS = 128
NNZ = 64
RING = 8
PAIRS = 6
SIB, FIRST, COMB, SECOND, GATHER1, GATHER2 = range(6)
SIB_FAR, SIB_NEAR, FAR, SUMS, LAST_SUMS, TOTAL, HALVES = range(7)


def loop(n, body):
    lax.fori_loop(0, n, lambda i, carry: (body(i), carry)[1], 0)


def kernel(
    feat, rows, cols, vals, w1_in, b1_in, w2_in, b2_in, out,
    v, x, a, h, s, agg, w1, b1, w2, b2, rows_v, cols_v, idx_v, idx,
    sib_out, sib_in, q, comb, t1, r1, f, fb, r2,
    sent, rs_recv, ag_recv, local_sem,
):
    row, col = lax.axis_index("row"), lax.axis_index("col")
    core, cx, cy = lax.rem(col, 2), lax.rem(col // 2, 4), col // 8

    def at(dz=0, dy=0, dx=0, other=False):
        yy, xx = lax.rem(cy + dy + 4, 4), lax.rem(cx + dx + 4, 4)
        kk = 1 - core if other else core
        return (lax.rem(row + dz + RING, RING), (yy * 4 + xx) * 2 + kk)

    sibling = at(other=True)
    along_z = {step: at(dz=step) for step in (1, -1, 2, -2)}
    along_x = {step: at(dx=step) for step in (1, 2, -1)}
    along_y = {step: at(dy=step) for step in (1, 2, -1)}
    ways = ((along_x, along_y), (along_y, along_x))
    barrier = pltpu.get_barrier_semaphore()
    peers = [sibling, *along_z.values(), *along_x.values(), *along_y.values()]
    for device in peers:
        pl.semaphore_signal(barrier, inc=1, device_id=device, device_id_type=MESH)

    loads = []
    for i, (src, dst) in enumerate((
        (feat, x.at[0]), (rows, rows_v), (cols, cols_v), (vals, v), (w1_in, w1), (b1_in, b1), (w2_in, w2), (b2_in, b2),
    )):
        loads.append(pltpu.make_async_copy(src, dst, local_sem.at[i]))
        loads[-1].start()

    def send(src, dst, kind, recv_sem, device):
        pltpu.make_async_remote_copy(
            src_ref=src, dst_ref=dst, send_sem=sent.at[kind], recv_sem=recv_sem,
            device_id=device, device_id_type=MESH,
        ).start()

    def arrived(ref, recv_sem):
        pltpu.make_async_remote_copy(
            src_ref=ref, dst_ref=ref, send_sem=sent.at[SIB], recv_sem=recv_sem,
            device_id=sibling, device_id_type=MESH,
        ).wait_recv()

    def all_sent(ref, kind):
        pltpu.make_async_remote_copy(
            src_ref=ref, dst_ref=ref, send_sem=sent.at[kind], recv_sem=rs_recv.at[0, 0],
            device_id=sibling, device_id_type=MESH,
        ).wait_send()

    def rounds(t):
        return (
            ((0, 1), (0, -1)),
            ((7, 1), (1, -1)),
            ((6, 2), (6, 1), (2, -1)) if t % 2 == 0 else ((2, -2), (2, -1), (6, 1)),
        )

    class Gather:
        def __init__(self, buf, layer, t):
            self.buf, self.kind, self.t, self.sems = buf, GATHER1 + layer, t, ag_recv.at[layer * 4 + t]

        def start(self, n, source):
            for slot_at, step in rounds(self.t)[n]:
                if slot_at == source:
                    target = (slot_at - step) % RING
                    send(self.buf.at[slot_at, self.t], self.buf.at[target, self.t], self.kind, self.sems.at[target - 1], along_z[step])

        def arrive(self, n):
            filled = [(slot_at - step) % RING for slot_at, step in rounds(self.t)[n]]
            if n == 2:
                filled.sort(key=lambda target: target == 4)
            for target in filled:
                arrived(self.buf.at[target, self.t], self.sems.at[target - 1])
                if n < 2:
                    self.start(n + 1, target)
            return filled

    loads[0].wait()
    pl.semaphore_wait(barrier, len(peers))
    first = [Gather(x, 0, t) for t in range(4)]
    for g in first:
        g.start(0, 0)
    loads[1].wait()
    loads[2].wait()
    wide = jnp.broadcast_to(rows_v[...], (NNZ, NNZ))
    sub = lax.broadcasted_iota(jnp.int32, (NNZ, NNZ), 0)
    lane = lax.broadcasted_iota(jnp.int32, (NNZ, NNZ), 1)
    tall = jnp.sum(jnp.where(sub == lane, wide, 0), axis=1, keepdims=True)
    before = jnp.max(jnp.where((tall == wide) & (sub < lane), sub, -1), axis=0, keepdims=True)
    sub = lax.broadcasted_iota(jnp.int32, (NNZ, BS), 0)
    lane = lax.broadcasted_iota(jnp.int32, (NNZ, BS), 1)
    last = jnp.max(jnp.where(tall == lane, sub, -1), axis=0, keepdims=True)
    held = cols_v[...]
    slot = (((held >> 2) - row + RING) & (RING - 1)) * 4 + (held & 3)
    idx_v[...] = jnp.zeros_like(idx_v)
    idx_v[0:1, :] = jnp.where(last < 0, NNZ, last)
    idx_v[1:2, 0:NNZ] = jnp.where(before < 0, NNZ, before)
    idx_v[2:3, 0:NNZ] = slot
    to_scalars = pltpu.make_async_copy(idx_v, idx, local_sem.at[8])
    to_scalars.start()
    s[0, NNZ] = jnp.zeros((BS, BS), F32)
    s[1, NNZ] = jnp.zeros((BS, BS), F32)

    for n in range(3):
        for g in first:
            g.arrive(n)
    for copy in loads[3:]:
        copy.wait()
    to_scalars.wait()

    def products(half, source):
        for e in range(NNZ):
            held = source(idx[2, e])
            s[half, e] = jnp.dot(v[e], held, preferred_element_type=F32) + s[half, idx[1, e]]

    class Pair:
        def __init__(self, number, half, j):
            self.p, self.half, self.j, self.sems = number, half, j, rs_recv.at[number]

        def own(self, w, d, g, kk):
            if w == 0:
                xx, yy = (cx + d) & 3, (cy + g) & 3
            else:
                yy, xx = (cy + d) & 3, (cx + g) & 3
            b = ((yy * 4 + xx) * 2 + kk) * 4 + self.j * 2 + w
            return s[self.half, idx[0, b]]

        def chip(self, w, d, e, g):
            return self.own(w, d, g, core) + sib_in[self.p, e, w, g].astype(F32)

        def to_sibling(self, e, d, step, n, sem):
            p = self.p
            for w in range(2):

                def body(i):
                    for g in range(4):
                        sib_out[p, e + i, w, g] = self.own(w, d + step * i, g, 1 - core).astype(BF)

                loop(n, body)
            part = pl.ds(e, n)
            send(sib_out.at[p, part], sib_in.at[p, part], SIB, self.sems.at[sem], sibling)

        def sib_far(self):
            self.to_sibling(0, 2, 0, 1, SIB_FAR)

        def sib_near(self):
            self.to_sibling(1, 1, 2, 2, SIB_NEAR)

        def sib_here(self):
            self.to_sibling(3, 0, 0, 1, SUMS)

        def far(self):
            p = self.p
            arrived(sib_in.at[p, 0], self.sems.at[SIB_FAR])
            for w in range(2):

                def body(g):
                    q[p, w, g] = self.chip(w, 2, 0, g).astype(BF)

                loop(4, body)
                for at_q, step in ((0, 1), (2, -1)):
                    part = pl.ds(at_q, 2)
                    send(q.at[p, w, part], t1.at[p, w, part], FIRST, self.sems.at[FAR], ways[w][0][step])

        def near(self):
            p = self.p
            arrived(sib_in.at[p, pl.ds(1, 2)], self.sems.at[SIB_NEAR])
            for w in range(2):

                def body(i):
                    q[p, w, 4 + i] = self.chip(w, 1 + 2 * (i // 2), 1 + i // 2, (i + 2) & 3).astype(BF)

                loop(4, body)
                for side, step in ((0, 1), (1, -1)):
                    send(
                        q.at[p, w, pl.ds(4 + 2 * side, 2)], r1.at[p, w, side, pl.ds(2 - 2 * side, 2)],
                        FIRST, self.sems.at[SUMS], ways[w][0][step],
                    )

        def passed(self):
            p = self.p
            arrived(t1.at[p], self.sems.at[FAR])
            for n, sem in ((1, SUMS), (0, LAST_SUMS)):
                for w in range(2):
                    for side, step in ((0, 1), (1, -1)):
                        g = 2 * side + n
                        held = self.chip(w, 1 + 2 * side, 1 + side, g)
                        comb[p, w, g] = (held + t1[p, w, g].astype(F32)).astype(BF)
                        send(comb.at[p, w, g], r1.at[p, w, side, g], COMB, self.sems.at[sem], ways[w][0][step])

        def sums(self, w, g):
            p = self.p
            return self.chip(w, 0, 3, g) + (r1[p, w, 0, g].astype(F32) + r1[p, w, 1, g].astype(F32))

        def away(self, w, g):
            p = self.p
            fb[p, w, g - 1] = self.sums(w, g).astype(BF)
            send(fb.at[p, w, g - 1], r2.at[p, w, g - 1], SECOND, self.sems.at[TOTAL], ways[w][1][-1 if g == 3 else g])

        def second(self):
            p = self.p
            arrived(sib_in.at[pl.ds(0, 5), 0, 0], self.sems.at[SUMS])
            for g in (1, 3):
                for w in range(2):
                    self.away(w, g)
            arrived(r1.at[p, 0, 0], self.sems.at[LAST_SUMS])
            for w in range(2):
                self.away(w, 2)
            for w in range(2):
                f[p, w] = self.sums(w, 0)

        def part_way(self, src, dst, rows, sem, step):
            send(fb.at[self.p, *src, rows], r2.at[self.p, *dst, rows], SECOND, self.sems.at[sem], ways[src[0]][1][step])

        def second_halves(self):
            p, upper, lower = self.p, pl.ds(0, 64), pl.ds(64, 64)
            arrived(sib_in.at[pl.ds(0, 5), 0, 0], self.sems.at[SUMS])
            arrived(r1.at[p, 0, 0], self.sems.at[LAST_SUMS])
            for w in range(2):
                fb[p, w, 0] = self.sums(w, 2).astype(BF)
                self.part_way((w, 0), (w, 2), upper, HALVES, 1)
                self.part_way((w, 0), (w, 2), lower, HALVES, -1)
            for w in range(2):
                fb[p, w, 1, 64:128] = self.sums(w, 1)[64:128].astype(BF)
                self.part_way((w, 1), (w, 0), lower, TOTAL, 1)
                fb[p, w, 1, 0:64] = self.sums(w, 3)[0:64].astype(BF)
                self.part_way((w, 1), (w, 1), upper, TOTAL, -1)
                f[p, w] = self.sums(w, 0)

        def third(self):
            p, upper, lower = self.p, pl.ds(0, 64), pl.ds(64, 64)
            arrived(fb.at[p, 0, pl.ds(0, 2)], self.sems.at[HALVES])
            for w in range(2):
                fb[p, w, 2, 0:64] = (self.sums(w, 1)[0:64] + r2[p, w, 2, 0:64].astype(F32)).astype(BF)
                self.part_way((w, 2), (w, 0), upper, TOTAL, 1)
                fb[p, w, 2, 64:128] = (self.sums(w, 3)[64:128] + r2[p, w, 2, 64:128].astype(F32)).astype(BF)
                self.part_way((w, 2), (w, 1), lower, TOTAL, -1)

        def total_halves(self):
            p = self.p
            arrived(r1.at[p, 0, 0], self.sems.at[TOTAL])
            return [(f[p, w] + (r2[p, w, 0].astype(F32) + r2[p, w, 1].astype(F32))).astype(BF) for w in range(2)]

        def total(self):
            p = self.p
            arrived(r2.at[p], self.sems.at[TOTAL])
            return [
                (f[p, w] + r2[p, w, 0].astype(F32) + (r2[p, w, 1].astype(F32) + r2[p, w, 2].astype(F32))).astype(BF)
                for w in range(2)
            ]

    def hidden(n, t):
        made = jnp.dot(a[n, t], w1[...], preferred_element_type=F32) + b1[...]
        made = jnp.maximum(made, 0.0).astype(BF)
        h[0, n * 4 + t] = made[:, :BS]
        h[1, n * 4 + t] = made[:, BS:]

    products(0, lambda n: x[n // 4, n % 4])
    pairs = [Pair(j, 0, j) for j in range(2)]
    gathers = [Gather(a, 1, t) for t in range(4)]

    def publish(j):
        for w, block in enumerate(pairs[j].total()):
            a[0, 2 * j + w] = block
            gathers[2 * j + w].start(0, 0)
        for w in range(2):
            hidden(0, 2 * j + w)

    def arrive(n, j):
        filled = [(t, slot_at) for t in (2 * j, 2 * j + 1) for slot_at in gathers[t].arrive(n)]
        for t, slot_at in filled:
            hidden(slot_at, t)

    one, two = pairs
    one.sib_far()
    two.sib_far()
    one.sib_near()
    two.sib_near()
    one.sib_here()
    two.sib_here()
    one.far()
    two.far()
    one.near()
    one.passed()
    two.near()
    two.passed()
    one.second()
    two.second()
    publish(0)
    publish(1)
    for n in range(3):
        arrive(n, 0)
        arrive(n, 1)

    pairs = [Pair(2 + i, i // 2, i % 2) for i in range(4)]

    def finish(pair):
        for w, block in enumerate(pair.total() if pair is four else pair.total_halves()):
            agg[2 * pair.j + w, :, pair.half * BS : (pair.half + 1) * BS] = block

    one, two, three, four = pairs
    products(0, lambda n: h[0, n])
    one.sib_far()
    two.sib_far()
    one.sib_near()
    two.sib_near()
    one.sib_here()
    two.sib_here()
    one.far()
    two.far()
    one.near()
    products(1, lambda n: h[1, n])
    three.sib_far()
    four.sib_far()
    three.sib_near()
    four.sib_near()
    three.sib_here()
    four.sib_here()
    one.passed()
    two.near()
    three.far()
    two.passed()
    three.near()
    four.far()
    three.passed()
    four.near()
    four.passed()
    one.second_halves()
    two.second_halves()
    three.second_halves()
    one.third()
    two.third()
    four.second()
    three.third()
    finish(one)
    finish(two)

    def put(t):
        made = jnp.dot(agg[t], w2[...], preferred_element_type=F32) + b2[...]
        out[t] = jnp.maximum(made, 0.0).astype(BF)

    finish(three)
    put(0)
    put(1)
    finish(four)
    put(2)
    put(3)
    all_sent(sib_out, SIB)
    all_sent(q, FIRST)
    all_sent(comb, COMB)
    all_sent(fb, SECOND)
    all_sent(x.at[pl.ds(1, 7)], GATHER1)
    all_sent(a.at[pl.ds(1, 7)], GATHER2)


def local(features, block_rows, block_cols, block_values, weight_one, bias_one, weight_two, bias_two):
    block = (BS, BS)
    return pl.pallas_call(
        kernel,
        out_shape=pltpu.VMEM((4, BS, 2 * BS), BF),
        in_specs=[pl.BlockSpec(memory_space=pl.ANY)] * 8,
        out_specs=pl.BlockSpec(memory_space=pltpu.VMEM),
        scratch_shapes=[
            pltpu.VMEM((NNZ, *block), BF),
            pltpu.VMEM((RING, 4, *block), BF),
            pltpu.VMEM((RING, 4, *block), BF),
            pltpu.VMEM((2, RING * 4, *block), BF),
            pltpu.VMEM((2, NNZ + 1, *block), F32),
            pltpu.VMEM((4, BS, 2 * BS), BF),
            pltpu.VMEM((128, 256), BF),
            pltpu.VMEM((1, 256), F32),
            pltpu.VMEM((256, 256), BF),
            pltpu.VMEM((1, 256), F32),
            pltpu.VMEM((1, NNZ), jnp.int32),
            pltpu.VMEM((1, NNZ), jnp.int32),
            pltpu.VMEM((8, BS), jnp.int32),
            pltpu.SMEM((8, BS), jnp.int32),
            pltpu.VMEM((PAIRS, 4, 2, 4, *block), BF),
            pltpu.VMEM((PAIRS, 4, 2, 4, *block), BF),
            pltpu.VMEM((PAIRS, 2, 8, *block), BF),
            pltpu.VMEM((PAIRS, 2, 4, *block), BF),
            pltpu.VMEM((PAIRS, 2, 4, *block), BF),
            pltpu.VMEM((PAIRS, 2, 2, 4, *block), BF),
            pltpu.VMEM((PAIRS, 2, *block), F32),
            pltpu.VMEM((PAIRS, 2, 3, *block), BF),
            pltpu.VMEM((PAIRS, 2, 3, *block), BF),
            pltpu.SemaphoreType.DMA((6,)),
            pltpu.SemaphoreType.DMA((PAIRS, 7)),
            pltpu.SemaphoreType.DMA((8, 7)),
            pltpu.SemaphoreType.DMA((9,)),
        ],
        compiler_params=pltpu.CompilerParams(
            collective_id=1, has_side_effects=True, vmem_limit_bytes=56 * 2**20
        ),
        name="two_layers",
    )(
        features.reshape(4, *block),
        block_rows.reshape(1, NNZ),
        block_cols.reshape(1, NNZ),
        block_values.reshape(NNZ, *block),
        weight_one,
        bias_one.reshape(1, -1),
        weight_two,
        bias_two.reshape(1, -1),
    ).reshape(512, 256)


def solution(mesh):
    placed = (
        P(("row", "col"), None),
        P("row", "col", None),
        P("row", "col", None),
        P("row", "col", None, None, None),
        P(),
        P(),
        P(),
        P(),
    )
    return jax.shard_map(
        local, mesh=mesh, in_specs=placed, out_specs=P(("row", "col"), None), check_vma=False
    )
```

```python
import functools

import jax
import jax.numpy as jnp
from jax import lax
from jax.experimental import pallas as pl
from jax.experimental.pallas import tpu as pltpu
from jax.sharding import PartitionSpec as P

MESH = pl.DeviceIdType.MESH
BF = jnp.bfloat16
F32 = jnp.float32
BS = 128
NNZ = 64
RING = 8
PAIRS = 6
SIB, FIRST, COMB, SECOND, GATHER1, GATHER2 = range(6)
SIB_FAR, SIB_NEAR, FAR, SUMS, LAST_SUMS, TOTAL, HALVES = range(7)


def loop(n, body):
    lax.fori_loop(0, n, lambda i, carry: (body(i), carry)[1], 0)


def kernel(
    feat, rows, cols, vals, w1_in, b1_in, w2_in, b2_in, out,
    v, x, a, h, s, agg, w1, b1, w2, b2, rows_v, cols_v, idx_v, idx,
    sib_out, sib_in, q, comb, t1, r1, f, fb, r2,
    sent, rs_recv, ag_recv, local_sem,
):
    row, col = lax.axis_index("row"), lax.axis_index("col")
    core, cx, cy = lax.rem(col, 2), lax.rem(col // 2, 4), col // 8

    def at(dz=0, dy=0, dx=0, other=False):
        yy, xx = lax.rem(cy + dy + 4, 4), lax.rem(cx + dx + 4, 4)
        kk = 1 - core if other else core
        return (lax.rem(row + dz + RING, RING), (yy * 4 + xx) * 2 + kk)

    sibling = at(other=True)
    along_z = {step: at(dz=step) for step in (1, -1, 2, -2)}
    along_x = {step: at(dx=step) for step in (1, 2, -1)}
    along_y = {step: at(dy=step) for step in (1, 2, -1)}
    ways = ((along_x, along_y), (along_y, along_x))
    barrier = pltpu.get_barrier_semaphore()
    peers = [sibling, *along_z.values(), *along_x.values(), *along_y.values()]
    for device in peers:
        pl.semaphore_signal(barrier, inc=1, device_id=device, device_id_type=MESH)

    loads = []
    for i, (src, dst) in enumerate((
        (feat, x.at[0]), (rows, rows_v), (cols, cols_v), (vals, v), (w1_in, w1), (b1_in, b1), (w2_in, w2), (b2_in, b2),
    )):
        loads.append(pltpu.make_async_copy(src, dst, local_sem.at[i]))
        loads[-1].start()

    def send(src, dst, kind, recv_sem, device):
        pltpu.make_async_remote_copy(
            src_ref=src, dst_ref=dst, send_sem=sent.at[kind], recv_sem=recv_sem,
            device_id=device, device_id_type=MESH,
        ).start()

    def arrived(ref, recv_sem):
        pltpu.make_async_remote_copy(
            src_ref=ref, dst_ref=ref, send_sem=sent.at[SIB], recv_sem=recv_sem,
            device_id=sibling, device_id_type=MESH,
        ).wait_recv()

    def all_sent(ref, kind):
        pltpu.make_async_remote_copy(
            src_ref=ref, dst_ref=ref, send_sem=sent.at[kind], recv_sem=rs_recv.at[0, 0],
            device_id=sibling, device_id_type=MESH,
        ).wait_send()

    def rounds(t):
        return (
            ((0, 1), (0, -1)),
            ((7, 1), (1, -1)),
            ((6, 2), (6, 1), (2, -1)) if t % 2 == 0 else ((2, -2), (2, -1), (6, 1)),
        )

    class Gather:
        def __init__(self, buf, layer, t):
            self.buf, self.kind, self.t, self.sems = buf, GATHER1 + layer, t, ag_recv.at[layer * 4 + t]

        def start(self, n, source):
            for slot_at, step in rounds(self.t)[n]:
                if slot_at == source:
                    target = (slot_at - step) % RING
                    send(self.buf.at[slot_at, self.t], self.buf.at[target, self.t], self.kind, self.sems.at[target - 1], along_z[step])

        def arrive(self, n):
            filled = [(slot_at - step) % RING for slot_at, step in rounds(self.t)[n]]
            if n == 2:
                filled.sort(key=lambda target: target == 4)
            for target in filled:
                arrived(self.buf.at[target, self.t], self.sems.at[target - 1])
                if n < 2:
                    self.start(n + 1, target)
            return filled

    loads[0].wait()
    pl.semaphore_wait(barrier, len(peers))
    first = [Gather(x, 0, t) for t in range(4)]
    for g in first:
        g.start(0, 0)
    loads[1].wait()
    loads[2].wait()
    wide = jnp.broadcast_to(rows_v[...], (NNZ, NNZ))
    sub = lax.broadcasted_iota(jnp.int32, (NNZ, NNZ), 0)
    lane = lax.broadcasted_iota(jnp.int32, (NNZ, NNZ), 1)
    tall = jnp.sum(jnp.where(sub == lane, wide, 0), axis=1, keepdims=True)
    before = jnp.max(jnp.where((tall == wide) & (sub < lane), sub, -1), axis=0, keepdims=True)
    sub = lax.broadcasted_iota(jnp.int32, (NNZ, BS), 0)
    lane = lax.broadcasted_iota(jnp.int32, (NNZ, BS), 1)
    last = jnp.max(jnp.where(tall == lane, sub, -1), axis=0, keepdims=True)
    held = cols_v[...]
    slot = (((held >> 2) - row + RING) & (RING - 1)) * 4 + (held & 3)
    idx_v[...] = jnp.zeros_like(idx_v)
    idx_v[0:1, :] = jnp.where(last < 0, NNZ, last)
    idx_v[1:2, 0:NNZ] = jnp.where(before < 0, NNZ, before)
    idx_v[2:3, 0:NNZ] = slot
    to_scalars = pltpu.make_async_copy(idx_v, idx, local_sem.at[8])
    to_scalars.start()
    s[0, NNZ] = jnp.zeros((BS, BS), F32)
    s[1, NNZ] = jnp.zeros((BS, BS), F32)

    for n in range(3):
        for g in first:
            g.arrive(n)
    for copy in loads[3:]:
        copy.wait()
    to_scalars.wait()

    def products(half, source):
        for e in range(NNZ):
            held = source(idx[2, e])
            s[half, e] = jnp.dot(v[e], held, preferred_element_type=F32) + s[half, idx[1, e]]

    class Pair:
        def __init__(self, number, half, j):
            self.p, self.half, self.j, self.sems = number, half, j, rs_recv.at[number]

        def own(self, w, d, g, kk):
            if w == 0:
                xx, yy = (cx + d) & 3, (cy + g) & 3
            else:
                yy, xx = (cy + d) & 3, (cx + g) & 3
            b = ((yy * 4 + xx) * 2 + kk) * 4 + self.j * 2 + w
            return s[self.half, idx[0, b]]

        def chip(self, w, d, e, g):
            return self.own(w, d, g, core) + sib_in[self.p, e, w, g].astype(F32)

        def to_sibling(self, e, d, step, n, sem):
            p = self.p
            for w in range(2):

                def body(i):
                    for g in range(4):
                        sib_out[p, e + i, w, g] = self.own(w, d + step * i, g, 1 - core).astype(BF)

                loop(n, body)
            part = pl.ds(e, n)
            send(sib_out.at[p, part], sib_in.at[p, part], SIB, self.sems.at[sem], sibling)

        def sib_far(self):
            self.to_sibling(0, 2, 0, 1, SIB_FAR)

        def sib_near(self):
            self.to_sibling(1, 1, 2, 2, SIB_NEAR)

        def sib_here(self):
            self.to_sibling(3, 0, 0, 1, SUMS)

        def far(self):
            p = self.p
            arrived(sib_in.at[p, 0], self.sems.at[SIB_FAR])
            for w in range(2):

                def body(g):
                    q[p, w, g] = self.chip(w, 2, 0, g).astype(BF)

                loop(4, body)
                for at_q, step in ((0, 1), (2, -1)):
                    part = pl.ds(at_q, 2)
                    send(q.at[p, w, part], t1.at[p, w, part], FIRST, self.sems.at[FAR], ways[w][0][step])

        def near(self):
            p = self.p
            arrived(sib_in.at[p, pl.ds(1, 2)], self.sems.at[SIB_NEAR])
            for w in range(2):

                def body(i):
                    q[p, w, 4 + i] = self.chip(w, 1 + 2 * (i // 2), 1 + i // 2, (i + 2) & 3).astype(BF)

                loop(4, body)
                for side, step in ((0, 1), (1, -1)):
                    send(
                        q.at[p, w, pl.ds(4 + 2 * side, 2)], r1.at[p, w, side, pl.ds(2 - 2 * side, 2)],
                        FIRST, self.sems.at[SUMS], ways[w][0][step],
                    )

        def passed(self):
            p = self.p
            arrived(t1.at[p], self.sems.at[FAR])
            for n, sem in ((1, SUMS), (0, LAST_SUMS)):
                for w in range(2):
                    for side, step in ((0, 1), (1, -1)):
                        g = 2 * side + n
                        held = self.chip(w, 1 + 2 * side, 1 + side, g)
                        comb[p, w, g] = (held + t1[p, w, g].astype(F32)).astype(BF)
                        send(comb.at[p, w, g], r1.at[p, w, side, g], COMB, self.sems.at[sem], ways[w][0][step])

        def sums(self, w, g):
            p = self.p
            return self.chip(w, 0, 3, g) + (r1[p, w, 0, g].astype(F32) + r1[p, w, 1, g].astype(F32))

        def away(self, w, g):
            p = self.p
            fb[p, w, g - 1] = self.sums(w, g).astype(BF)
            send(fb.at[p, w, g - 1], r2.at[p, w, g - 1], SECOND, self.sems.at[TOTAL], ways[w][1][-1 if g == 3 else g])

        def second(self):
            p = self.p
            arrived(sib_in.at[pl.ds(0, 5), 0, 0], self.sems.at[SUMS])
            for g in (1, 3):
                for w in range(2):
                    self.away(w, g)
            arrived(r1.at[p, 0, 0], self.sems.at[LAST_SUMS])
            for w in range(2):
                self.away(w, 2)
            for w in range(2):
                f[p, w] = self.sums(w, 0)

        def part_way(self, src, dst, rows, sem, step):
            send(fb.at[self.p, *src, rows], r2.at[self.p, *dst, rows], SECOND, self.sems.at[sem], ways[src[0]][1][step])

        def second_halves(self):
            p, upper, lower = self.p, pl.ds(0, 64), pl.ds(64, 64)
            arrived(sib_in.at[pl.ds(0, 5), 0, 0], self.sems.at[SUMS])
            arrived(r1.at[p, 0, 0], self.sems.at[LAST_SUMS])
            for w in range(2):
                fb[p, w, 0] = self.sums(w, 2).astype(BF)
                self.part_way((w, 0), (w, 2), upper, HALVES, 1)
                self.part_way((w, 0), (w, 2), lower, HALVES, -1)
            for w in range(2):
                fb[p, w, 1, 64:128] = self.sums(w, 1)[64:128].astype(BF)
                self.part_way((w, 1), (w, 0), lower, TOTAL, 1)
                fb[p, w, 1, 0:64] = self.sums(w, 3)[0:64].astype(BF)
                self.part_way((w, 1), (w, 1), upper, TOTAL, -1)
                f[p, w] = self.sums(w, 0)

        def third(self):
            p, upper, lower = self.p, pl.ds(0, 64), pl.ds(64, 64)
            arrived(fb.at[p, 0, pl.ds(0, 2)], self.sems.at[HALVES])
            for w in range(2):
                fb[p, w, 2, 0:64] = (self.sums(w, 1)[0:64] + r2[p, w, 2, 0:64].astype(F32)).astype(BF)
                self.part_way((w, 2), (w, 0), upper, TOTAL, 1)
                fb[p, w, 2, 64:128] = (self.sums(w, 3)[64:128] + r2[p, w, 2, 64:128].astype(F32)).astype(BF)
                self.part_way((w, 2), (w, 1), lower, TOTAL, -1)

        def total_halves(self):
            p = self.p
            arrived(r1.at[p, 0, 0], self.sems.at[TOTAL])
            return [(f[p, w] + (r2[p, w, 0].astype(F32) + r2[p, w, 1].astype(F32))).astype(BF) for w in range(2)]

        def total(self):
            p = self.p
            arrived(r2.at[p], self.sems.at[TOTAL])
            return [
                (f[p, w] + r2[p, w, 0].astype(F32) + (r2[p, w, 1].astype(F32) + r2[p, w, 2].astype(F32))).astype(BF)
                for w in range(2)
            ]

    def hidden(n, t):
        made = jnp.dot(a[n, t], w1[...], preferred_element_type=F32) + b1[...]
        made = jnp.maximum(made, 0.0).astype(BF)
        h[0, n * 4 + t] = made[:, :BS]
        h[1, n * 4 + t] = made[:, BS:]

    products(0, lambda n: x[n // 4, n % 4])
    pairs = [Pair(j, 0, j) for j in range(2)]
    gathers = [Gather(a, 1, t) for t in range(4)]

    def publish(j):
        for w, block in enumerate(pairs[j].total()):
            a[0, 2 * j + w] = block
            gathers[2 * j + w].start(0, 0)
        for w in range(2):
            hidden(0, 2 * j + w)

    def arrive(n, j):
        filled = [(t, slot_at) for t in (2 * j, 2 * j + 1) for slot_at in gathers[t].arrive(n)]
        for t, slot_at in filled:
            hidden(slot_at, t)

    one, two = pairs
    one.sib_far()
    two.sib_far()
    one.sib_near()
    two.sib_near()
    one.sib_here()
    two.sib_here()
    one.far()
    two.far()
    one.near()
    one.passed()
    two.near()
    two.passed()
    one.second()
    two.second()
    publish(0)
    publish(1)
    for n in range(3):
        arrive(n, 0)
        arrive(n, 1)

    pairs = [Pair(2 + i, i // 2, i % 2) for i in range(4)]

    def finish(pair):
        for w, block in enumerate(pair.total() if pair in (three, four,) else pair.total_halves()):
            agg[2 * pair.j + w, :, pair.half * BS : (pair.half + 1) * BS] = block

    one, two, three, four = pairs
    products(0, lambda n: h[0, n])
    one.sib_far()
    two.sib_far()
    one.sib_near()
    two.sib_near()
    one.sib_here()
    two.sib_here()
    one.far()
    two.far()
    one.near()
    products(1, lambda n: h[1, n])
    three.sib_far()
    four.sib_far()
    three.sib_near()
    four.sib_near()
    three.sib_here()
    four.sib_here()
    one.passed()
    two.near()
    three.far()
    two.passed()
    three.near()
    four.far()
    three.passed()
    four.near()
    four.passed()
    one.second_halves()
    two.second_halves()
    three.second()
    one.third()
    four.second()
    two.third()
    finish(one)
    finish(two)

    def put(t):
        made = jnp.dot(agg[t], w2[...], preferred_element_type=F32) + b2[...]
        out[t] = jnp.maximum(made, 0.0).astype(BF)

    finish(three)
    put(0)
    put(1)
    finish(four)
    put(2)
    put(3)
    all_sent(sib_out, SIB)
    all_sent(q, FIRST)
    all_sent(comb, COMB)
    all_sent(fb, SECOND)
    all_sent(x.at[pl.ds(1, 7)], GATHER1)
    all_sent(a.at[pl.ds(1, 7)], GATHER2)


def local(features, block_rows, block_cols, block_values, weight_one, bias_one, weight_two, bias_two):
    block = (BS, BS)
    return pl.pallas_call(
        kernel,
        out_shape=pltpu.VMEM((4, BS, 2 * BS), BF),
        in_specs=[pl.BlockSpec(memory_space=pl.ANY)] * 8,
        out_specs=pl.BlockSpec(memory_space=pltpu.VMEM),
        scratch_shapes=[
            pltpu.VMEM((NNZ, *block), BF),
            pltpu.VMEM((RING, 4, *block), BF),
            pltpu.VMEM((RING, 4, *block), BF),
            pltpu.VMEM((2, RING * 4, *block), BF),
            pltpu.VMEM((2, NNZ + 1, *block), F32),
            pltpu.VMEM((4, BS, 2 * BS), BF),
            pltpu.VMEM((128, 256), BF),
            pltpu.VMEM((1, 256), F32),
            pltpu.VMEM((256, 256), BF),
            pltpu.VMEM((1, 256), F32),
            pltpu.VMEM((1, NNZ), jnp.int32),
            pltpu.VMEM((1, NNZ), jnp.int32),
            pltpu.VMEM((8, BS), jnp.int32),
            pltpu.SMEM((8, BS), jnp.int32),
            pltpu.VMEM((PAIRS, 4, 2, 4, *block), BF),
            pltpu.VMEM((PAIRS, 4, 2, 4, *block), BF),
            pltpu.VMEM((PAIRS, 2, 8, *block), BF),
            pltpu.VMEM((PAIRS, 2, 4, *block), BF),
            pltpu.VMEM((PAIRS, 2, 4, *block), BF),
            pltpu.VMEM((PAIRS, 2, 2, 4, *block), BF),
            pltpu.VMEM((PAIRS, 2, *block), F32),
            pltpu.VMEM((PAIRS, 2, 3, *block), BF),
            pltpu.VMEM((PAIRS, 2, 3, *block), BF),
            pltpu.SemaphoreType.DMA((6,)),
            pltpu.SemaphoreType.DMA((PAIRS, 7)),
            pltpu.SemaphoreType.DMA((8, 7)),
            pltpu.SemaphoreType.DMA((9,)),
        ],
        compiler_params=pltpu.CompilerParams(
            collective_id=1, has_side_effects=True, vmem_limit_bytes=56 * 2**20
        ),
        name="two_layers",
    )(
        features.reshape(4, *block),
        block_rows.reshape(1, NNZ),
        block_cols.reshape(1, NNZ),
        block_values.reshape(NNZ, *block),
        weight_one,
        bias_one.reshape(1, -1),
        weight_two,
        bias_two.reshape(1, -1),
    ).reshape(512, 256)


def solution(mesh):
    placed = (
        P(("row", "col"), None),
        P("row", "col", None),
        P("row", "col", None),
        P("row", "col", None, None, None),
        P(),
        P(),
        P(),
        P(),
    )
    return jax.shard_map(
        local, mesh=mesh, in_specs=placed, out_specs=P(("row", "col"), None), check_vma=False
    )
```

```python
import functools

import jax
import jax.numpy as jnp
from jax import lax
from jax.experimental import pallas as pl
from jax.experimental.pallas import tpu as pltpu
from jax.sharding import PartitionSpec as P

MESH = pl.DeviceIdType.MESH
BF = jnp.bfloat16
F32 = jnp.float32
BS = 128
NNZ = 64
RING = 8
PAIRS = 6
SIB, FIRST, COMB, SECOND, GATHER1, GATHER2 = range(6)
SIB_FAR, SIB_NEAR, FAR, SUMS, LAST_SUMS, TOTAL, HALVES = range(7)


def loop(n, body):
    lax.fori_loop(0, n, lambda i, carry: (body(i), carry)[1], 0)


def kernel(
    feat, rows, cols, vals, w1_in, b1_in, w2_in, b2_in, out,
    v, x, a, h, s, agg, w1, b1, w2, b2, rows_v, cols_v, idx_v, idx,
    sib_out, sib_in, q, comb, t1, r1, f, fb, r2,
    sent, rs_recv, ag_recv, ag_last, local_sem,
):
    row, col = lax.axis_index("row"), lax.axis_index("col")
    core, cx, cy = lax.rem(col, 2), lax.rem(col // 2, 4), col // 8

    def at(dz=0, dy=0, dx=0, other=False):
        yy, xx = lax.rem(cy + dy + 4, 4), lax.rem(cx + dx + 4, 4)
        kk = 1 - core if other else core
        return (lax.rem(row + dz + RING, RING), (yy * 4 + xx) * 2 + kk)

    sibling = at(other=True)
    along_z = {step: at(dz=step) for step in (1, -1, 2, -2)}
    along_x = {step: at(dx=step) for step in (1, 2, -1)}
    along_y = {step: at(dy=step) for step in (1, 2, -1)}
    ways = ((along_x, along_y), (along_y, along_x))
    barrier = pltpu.get_barrier_semaphore()
    peers = [sibling, *along_z.values(), *along_x.values(), *along_y.values()]
    for device in peers:
        pl.semaphore_signal(barrier, inc=1, device_id=device, device_id_type=MESH)

    loads = []
    for i, (src, dst) in enumerate((
        (feat, x.at[0]), (rows, rows_v), (cols, cols_v), (vals, v), (w1_in, w1), (b1_in, b1), (w2_in, w2), (b2_in, b2),
    )):
        loads.append(pltpu.make_async_copy(src, dst, local_sem.at[i]))
        loads[-1].start()

    def send(src, dst, kind, recv_sem, device):
        pltpu.make_async_remote_copy(
            src_ref=src, dst_ref=dst, send_sem=sent.at[kind], recv_sem=recv_sem,
            device_id=device, device_id_type=MESH,
        ).start()

    def arrived(ref, recv_sem):
        pltpu.make_async_remote_copy(
            src_ref=ref, dst_ref=ref, send_sem=sent.at[SIB], recv_sem=recv_sem,
            device_id=sibling, device_id_type=MESH,
        ).wait_recv()

    def all_sent(ref, kind):
        pltpu.make_async_remote_copy(
            src_ref=ref, dst_ref=ref, send_sem=sent.at[kind], recv_sem=rs_recv.at[0, 0],
            device_id=sibling, device_id_type=MESH,
        ).wait_send()

    def rounds(t):
        return (
            ((0, 1), (0, -1)),
            ((7, 1), (1, -1)),
            ((6, 2), (6, 1), (2, -1)) if t % 2 == 0 else ((2, -2), (2, -1), (6, 1)),
        )

    class Gather:
        def __init__(self, buf, layer, t):
            self.buf, self.kind, self.t, self.sems = buf, GATHER1 + layer, t, ag_recv.at[layer * 4 + t]
            self.last_sem = ag_last.at[0 if layer == 0 else 1 + t // 2]

        def start(self, n, source):
            for slot_at, step in rounds(self.t)[n]:
                if slot_at == source:
                    target = (slot_at - step) % RING
                    sem = self.last_sem if n == 2 else self.sems.at[(7, 1, 6, 2).index(target)]
                    send(self.buf.at[slot_at, self.t], self.buf.at[target, self.t], self.kind, sem, along_z[step])

        def arrive(self, n):
            filled = [(slot_at - step) % RING for slot_at, step in rounds(self.t)[n]]
            if n < 2:
                for target in filled:
                    arrived(self.buf.at[target, self.t], self.sems.at[(7, 1, 6, 2).index(target)])
                    self.start(n + 1, target)
            return filled

    loads[0].wait()
    pl.semaphore_wait(barrier, len(peers))
    first = [Gather(x, 0, t) for t in range(4)]
    for g in first:
        g.start(0, 0)
    loads[1].wait()
    loads[2].wait()
    wide = jnp.broadcast_to(rows_v[...], (NNZ, NNZ))
    sub = lax.broadcasted_iota(jnp.int32, (NNZ, NNZ), 0)
    lane = lax.broadcasted_iota(jnp.int32, (NNZ, NNZ), 1)
    tall = jnp.sum(jnp.where(sub == lane, wide, 0), axis=1, keepdims=True)
    before = jnp.max(jnp.where((tall == wide) & (sub < lane), sub, -1), axis=0, keepdims=True)
    sub = lax.broadcasted_iota(jnp.int32, (NNZ, BS), 0)
    lane = lax.broadcasted_iota(jnp.int32, (NNZ, BS), 1)
    last = jnp.max(jnp.where(tall == lane, sub, -1), axis=0, keepdims=True)
    held = cols_v[...]
    slot = (((held >> 2) - row + RING) & (RING - 1)) * 4 + (held & 3)
    idx_v[...] = jnp.zeros_like(idx_v)
    idx_v[0:1, :] = jnp.where(last < 0, NNZ, last)
    idx_v[1:2, 0:NNZ] = jnp.where(before < 0, NNZ, before)
    idx_v[2:3, 0:NNZ] = slot
    to_scalars = pltpu.make_async_copy(idx_v, idx, local_sem.at[8])
    to_scalars.start()
    s[0, NNZ] = jnp.zeros((BS, BS), F32)
    s[1, NNZ] = jnp.zeros((BS, BS), F32)

    for n in range(2):
        for g in first:
            g.arrive(n)
    arrived(x.at[pl.ds(3, 3)], ag_last.at[0])
    for copy in loads[3:]:
        copy.wait()
    to_scalars.wait()

    def products(half, source):
        for e in range(NNZ):
            held = source(idx[2, e])
            s[half, e] = jnp.dot(v[e], held, preferred_element_type=F32) + s[half, idx[1, e]]

    class Pair:
        def __init__(self, number, half, j):
            self.p, self.half, self.j, self.sems = number, half, j, rs_recv.at[number]

        def own(self, w, d, g, kk):
            if w == 0:
                xx, yy = (cx + d) & 3, (cy + g) & 3
            else:
                yy, xx = (cy + d) & 3, (cx + g) & 3
            b = ((yy * 4 + xx) * 2 + kk) * 4 + self.j * 2 + w
            return s[self.half, idx[0, b]]

        def chip(self, w, d, e, g):
            return self.own(w, d, g, core) + sib_in[self.p, e, w, g].astype(F32)

        def to_sibling(self, e, d, step, n, sem):
            p = self.p
            for w in range(2):

                def body(i):
                    for g in range(4):
                        sib_out[p, e + i, w, g] = self.own(w, d + step * i, g, 1 - core).astype(BF)

                loop(n, body)
            part = pl.ds(e, n)
            send(sib_out.at[p, part], sib_in.at[p, part], SIB, self.sems.at[sem], sibling)

        def sib_far(self):
            self.to_sibling(0, 2, 0, 1, SIB_FAR)

        def sib_near(self):
            self.to_sibling(1, 1, 2, 2, SIB_NEAR)

        def sib_here(self):
            self.to_sibling(3, 0, 0, 1, SUMS)

        def far(self):
            p = self.p
            arrived(sib_in.at[p, 0], self.sems.at[SIB_FAR])
            for w in range(2):

                def body(g):
                    q[p, w, g] = self.chip(w, 2, 0, g).astype(BF)

                loop(4, body)
                for at_q, step in ((0, 1), (2, -1)):
                    part = pl.ds(at_q, 2)
                    send(q.at[p, w, part], t1.at[p, w, part], FIRST, self.sems.at[FAR], ways[w][0][step])

        def near(self):
            p = self.p
            arrived(sib_in.at[p, pl.ds(1, 2)], self.sems.at[SIB_NEAR])
            for w in range(2):

                def body(i):
                    q[p, w, 4 + i] = self.chip(w, 1 + 2 * (i // 2), 1 + i // 2, (i + 2) & 3).astype(BF)

                loop(4, body)
                for side, step in ((0, 1), (1, -1)):
                    send(
                        q.at[p, w, pl.ds(4 + 2 * side, 2)], r1.at[p, w, side, pl.ds(2 - 2 * side, 2)],
                        FIRST, self.sems.at[SUMS], ways[w][0][step],
                    )

        def passed(self):
            p = self.p
            arrived(t1.at[p], self.sems.at[FAR])
            for n, sem in ((1, SUMS), (0, LAST_SUMS)):
                for w in range(2):
                    for side, step in ((0, 1), (1, -1)):
                        g = 2 * side + n
                        held = self.chip(w, 1 + 2 * side, 1 + side, g)
                        comb[p, w, g] = (held + t1[p, w, g].astype(F32)).astype(BF)
                        send(comb.at[p, w, g], r1.at[p, w, side, g], COMB, self.sems.at[sem], ways[w][0][step])

        def sums(self, w, g):
            p = self.p
            return self.chip(w, 0, 3, g) + (r1[p, w, 0, g].astype(F32) + r1[p, w, 1, g].astype(F32))

        def away(self, w, g):
            p = self.p
            fb[p, w, g - 1] = self.sums(w, g).astype(BF)
            send(fb.at[p, w, g - 1], r2.at[p, w, g - 1], SECOND, self.sems.at[TOTAL], ways[w][1][-1 if g == 3 else g])

        def second(self):
            p = self.p
            arrived(sib_in.at[pl.ds(0, 5), 0, 0], self.sems.at[SUMS])
            for g in (1, 3):
                for w in range(2):
                    self.away(w, g)
            arrived(r1.at[p, 0, 0], self.sems.at[LAST_SUMS])
            for w in range(2):
                self.away(w, 2)
            for w in range(2):
                f[p, w] = self.sums(w, 0)

        def part_way(self, src, dst, rows, sem, step):
            send(fb.at[self.p, *src, rows], r2.at[self.p, *dst, rows], SECOND, self.sems.at[sem], ways[src[0]][1][step])

        def second_halves(self):
            p, upper, lower = self.p, pl.ds(0, 64), pl.ds(64, 64)
            arrived(sib_in.at[pl.ds(0, 5), 0, 0], self.sems.at[SUMS])
            arrived(r1.at[p, 0, 0], self.sems.at[LAST_SUMS])
            for w in range(2):
                fb[p, w, 0] = self.sums(w, 2).astype(BF)
                self.part_way((w, 0), (w, 2), upper, HALVES, 1)
                self.part_way((w, 0), (w, 2), lower, HALVES, -1)
            for w in range(2):
                fb[p, w, 1, 64:128] = self.sums(w, 1)[64:128].astype(BF)
                self.part_way((w, 1), (w, 0), lower, TOTAL, 1)
                fb[p, w, 1, 0:64] = self.sums(w, 3)[0:64].astype(BF)
                self.part_way((w, 1), (w, 1), upper, TOTAL, -1)
                f[p, w] = self.sums(w, 0)

        def third(self):
            p, upper, lower = self.p, pl.ds(0, 64), pl.ds(64, 64)
            arrived(fb.at[p, 0, pl.ds(0, 2)], self.sems.at[HALVES])
            for w in range(2):
                fb[p, w, 2, 0:64] = (self.sums(w, 1)[0:64] + r2[p, w, 2, 0:64].astype(F32)).astype(BF)
                self.part_way((w, 2), (w, 0), upper, TOTAL, 1)
                fb[p, w, 2, 64:128] = (self.sums(w, 3)[64:128] + r2[p, w, 2, 64:128].astype(F32)).astype(BF)
                self.part_way((w, 2), (w, 1), lower, TOTAL, -1)

        def total_halves(self):
            p = self.p
            arrived(r1.at[p, 0, 0], self.sems.at[TOTAL])
            return [(f[p, w] + (r2[p, w, 0].astype(F32) + r2[p, w, 1].astype(F32))).astype(BF) for w in range(2)]

        def total(self):
            p = self.p
            arrived(r2.at[p], self.sems.at[TOTAL])
            return [
                (f[p, w] + r2[p, w, 0].astype(F32) + (r2[p, w, 1].astype(F32) + r2[p, w, 2].astype(F32))).astype(BF)
                for w in range(2)
            ]

    def hidden(n, t):
        made = jnp.dot(a[n, t], w1[...], preferred_element_type=F32) + b1[...]
        made = jnp.maximum(made, 0.0).astype(BF)
        h[0, n * 4 + t] = made[:, :BS]
        h[1, n * 4 + t] = made[:, BS:]

    products(0, lambda n: x[n // 4, n % 4])
    pairs = [Pair(j, 0, j) for j in range(2)]
    gathers = [Gather(a, 1, t) for t in range(4)]

    def publish(j):
        for w, block in enumerate(pairs[j].total()):
            a[0, 2 * j + w] = block
            gathers[2 * j + w].start(0, 0)
        for w in range(2):
            hidden(0, 2 * j + w)

    def arrive(n, j):
        if n == 2:
            arrived(r2.at[0], ag_last.at[1 + j])
        filled = [(t, slot_at) for t in (2 * j, 2 * j + 1) for slot_at in gathers[t].arrive(n)]
        for t, slot_at in filled:
            hidden(slot_at, t)

    one, two = pairs
    one.sib_far()
    two.sib_far()
    one.sib_near()
    two.sib_near()
    one.sib_here()
    two.sib_here()
    one.far()
    two.far()
    one.near()
    one.passed()
    two.near()
    two.passed()
    one.second()
    two.second()
    publish(0)
    publish(1)
    for n in range(3):
        arrive(n, 0)
        arrive(n, 1)

    pairs = [Pair(2 + i, i // 2, i % 2) for i in range(4)]

    def finish(pair):
        for w, block in enumerate(pair.total() if pair in (three, four,) else pair.total_halves()):
            agg[2 * pair.j + w, :, pair.half * BS : (pair.half + 1) * BS] = block

    one, two, three, four = pairs
    products(0, lambda n: h[0, n])
    one.sib_far()
    two.sib_far()
    one.sib_near()
    two.sib_near()
    one.sib_here()
    two.sib_here()
    one.far()
    two.far()
    one.near()
    products(1, lambda n: h[1, n])
    three.sib_far()
    four.sib_far()
    three.sib_near()
    four.sib_near()
    three.sib_here()
    four.sib_here()
    one.passed()
    two.near()
    three.far()
    two.passed()
    three.near()
    four.far()
    three.passed()
    four.near()
    four.passed()
    one.second_halves()
    two.second_halves()
    three.second()
    one.third()
    four.second()
    two.third()
    finish(one)
    finish(two)

    def put(t):
        made = jnp.dot(agg[t], w2[...], preferred_element_type=F32) + b2[...]
        out[t] = jnp.maximum(made, 0.0).astype(BF)

    finish(three)
    put(0)
    put(1)
    finish(four)
    put(2)
    put(3)
    all_sent(sib_out, SIB)
    all_sent(q, FIRST)
    all_sent(comb, COMB)
    all_sent(fb, SECOND)
    all_sent(x.at[pl.ds(1, 7)], GATHER1)
    all_sent(a.at[pl.ds(1, 7)], GATHER2)


def local(features, block_rows, block_cols, block_values, weight_one, bias_one, weight_two, bias_two):
    block = (BS, BS)
    return pl.pallas_call(
        kernel,
        out_shape=pltpu.VMEM((4, BS, 2 * BS), BF),
        in_specs=[pl.BlockSpec(memory_space=pl.ANY)] * 8,
        out_specs=pl.BlockSpec(memory_space=pltpu.VMEM),
        scratch_shapes=[
            pltpu.VMEM((NNZ, *block), BF),
            pltpu.VMEM((RING, 4, *block), BF),
            pltpu.VMEM((RING, 4, *block), BF),
            pltpu.VMEM((2, RING * 4, *block), BF),
            pltpu.VMEM((2, NNZ + 1, *block), F32),
            pltpu.VMEM((4, BS, 2 * BS), BF),
            pltpu.VMEM((128, 256), BF),
            pltpu.VMEM((1, 256), F32),
            pltpu.VMEM((256, 256), BF),
            pltpu.VMEM((1, 256), F32),
            pltpu.VMEM((1, NNZ), jnp.int32),
            pltpu.VMEM((1, NNZ), jnp.int32),
            pltpu.VMEM((8, BS), jnp.int32),
            pltpu.SMEM((8, BS), jnp.int32),
            pltpu.VMEM((PAIRS, 4, 2, 4, *block), BF),
            pltpu.VMEM((PAIRS, 4, 2, 4, *block), BF),
            pltpu.VMEM((PAIRS, 2, 8, *block), BF),
            pltpu.VMEM((PAIRS, 2, 4, *block), BF),
            pltpu.VMEM((PAIRS, 2, 4, *block), BF),
            pltpu.VMEM((PAIRS, 2, 2, 4, *block), BF),
            pltpu.VMEM((PAIRS, 2, *block), F32),
            pltpu.VMEM((PAIRS, 2, 3, *block), BF),
            pltpu.VMEM((PAIRS, 2, 3, *block), BF),
            pltpu.SemaphoreType.DMA((6,)),
            pltpu.SemaphoreType.DMA((PAIRS, 7)),
            pltpu.SemaphoreType.DMA((8, 4)),
            pltpu.SemaphoreType.DMA((3,)),
            pltpu.SemaphoreType.DMA((9,)),
        ],
        compiler_params=pltpu.CompilerParams(
            collective_id=1, has_side_effects=True, vmem_limit_bytes=56 * 2**20
        ),
        name="two_layers",
    )(
        features.reshape(4, *block),
        block_rows.reshape(1, NNZ),
        block_cols.reshape(1, NNZ),
        block_values.reshape(NNZ, *block),
        weight_one,
        bias_one.reshape(1, -1),
        weight_two,
        bias_two.reshape(1, -1),
    ).reshape(512, 256)


def solution(mesh):
    placed = (
        P(("row", "col"), None),
        P("row", "col", None),
        P("row", "col", None),
        P("row", "col", None, None, None),
        P(),
        P(),
        P(),
        P(),
    )
    return jax.shard_map(
        local, mesh=mesh, in_specs=placed, out_specs=P(("row", "col"), None), check_vma=False
    )
```

```python
import functools

import jax
import jax.numpy as jnp
from jax import lax
from jax.experimental import pallas as pl
from jax.experimental.pallas import tpu as pltpu
from jax.sharding import PartitionSpec as P

MESH = pl.DeviceIdType.MESH
BF = jnp.bfloat16
F32 = jnp.float32
BS = 128
NNZ = 64
RING = 8
PAIRS = 6
SIB, FIRST, COMB, SECOND, GATHER1, GATHER2 = range(6)
SIB_FAR, SIB_NEAR, FAR, SUMS, LAST_SUMS, TOTAL, HALVES = range(7)


def loop(n, body):
    lax.fori_loop(0, n, lambda i, carry: (body(i), carry)[1], 0)


def kernel(
    feat, rows, cols, vals, w1_in, b1_in, w2_in, b2_in, out,
    v, x, a, h, s, agg, w1, b1, w2, b2, rows_v, cols_v, idx_v, idx,
    sib_out, sib_in, q, comb, t1, r1, f, fb, r2,
    sent, rs_recv, ag_recv, ag_last, local_sem,
):
    row, col = lax.axis_index("row"), lax.axis_index("col")
    core, cx, cy = lax.rem(col, 2), lax.rem(col // 2, 4), col // 8

    def at(dz=0, dy=0, dx=0, other=False):
        yy, xx = lax.rem(cy + dy + 4, 4), lax.rem(cx + dx + 4, 4)
        kk = 1 - core if other else core
        return (lax.rem(row + dz + RING, RING), (yy * 4 + xx) * 2 + kk)

    sibling = at(other=True)
    along_z = {step: at(dz=step) for step in (1, -1, 2, -2)}
    along_x = {step: at(dx=step) for step in (1, 2, -1)}
    along_y = {step: at(dy=step) for step in (1, 2, -1)}
    ways = ((along_x, along_y), (along_y, along_x))
    barrier = pltpu.get_barrier_semaphore()
    peers = [sibling, *along_z.values(), *along_x.values(), *along_y.values()]
    for device in peers:
        pl.semaphore_signal(barrier, inc=1, device_id=device, device_id_type=MESH)

    loads = []
    for i, (src, dst) in enumerate((
        (feat, x.at[0]), (rows, rows_v), (cols, cols_v), (vals, v), (w1_in, w1), (b1_in, b1), (w2_in, w2), (b2_in, b2),
    )):
        loads.append(pltpu.make_async_copy(src, dst, local_sem.at[i]))
        loads[-1].start()

    def send(src, dst, kind, recv_sem, device):
        pltpu.make_async_remote_copy(
            src_ref=src, dst_ref=dst, send_sem=sent.at[kind], recv_sem=recv_sem,
            device_id=device, device_id_type=MESH,
        ).start()

    def arrived(ref, recv_sem):
        pltpu.make_async_remote_copy(
            src_ref=ref, dst_ref=ref, send_sem=sent.at[SIB], recv_sem=recv_sem,
            device_id=sibling, device_id_type=MESH,
        ).wait_recv()

    def all_sent(ref, kind):
        pltpu.make_async_remote_copy(
            src_ref=ref, dst_ref=ref, send_sem=sent.at[kind], recv_sem=rs_recv.at[0, 0],
            device_id=sibling, device_id_type=MESH,
        ).wait_send()

    def rounds(t):
        return (
            ((0, 1), (0, -1)),
            ((7, 1), (1, -1)),
            ((6, 2), (6, 1), (2, -1)) if t % 2 == 0 else ((2, -2), (2, -1), (6, 1)),
        )

    class Gather:
        def __init__(self, buf, layer, t):
            self.buf, self.kind, self.t, self.sems = buf, GATHER1 + layer, t, ag_recv.at[layer * 4 + t]
            self.last_sem = ag_last.at[0 if layer == 0 else 1 + t // 2]

        def start(self, n, source):
            for slot_at, step in rounds(self.t)[n]:
                if slot_at == source:
                    target = (slot_at - step) % RING
                    sem = self.last_sem if n == 2 else self.sems.at[(7, 1, 6, 2).index(target)]
                    send(self.buf.at[slot_at, self.t], self.buf.at[target, self.t], self.kind, sem, along_z[step])

        def arrive(self, n):
            filled = [(slot_at - step) % RING for slot_at, step in rounds(self.t)[n]]
            if n < 2:
                for target in filled:
                    arrived(self.buf.at[target, self.t], self.sems.at[(7, 1, 6, 2).index(target)])
                    self.start(n + 1, target)
            return filled

    loads[0].wait()
    pl.semaphore_wait(barrier, len(peers))
    first = [Gather(x, 0, t) for t in range(4)]
    for g in first:
        g.start(0, 0)
    loads[1].wait()
    loads[2].wait()
    wide = jnp.broadcast_to(rows_v[...], (NNZ, NNZ))
    sub = lax.broadcasted_iota(jnp.int32, (NNZ, NNZ), 0)
    lane = lax.broadcasted_iota(jnp.int32, (NNZ, NNZ), 1)
    tall = jnp.sum(jnp.where(sub == lane, wide, 0), axis=1, keepdims=True)
    before = jnp.max(jnp.where((tall == wide) & (sub < lane), sub, -1), axis=0, keepdims=True)
    sub = lax.broadcasted_iota(jnp.int32, (NNZ, BS), 0)
    lane = lax.broadcasted_iota(jnp.int32, (NNZ, BS), 1)
    last = jnp.max(jnp.where(tall == lane, sub, -1), axis=0, keepdims=True)
    held = cols_v[...]
    slot = (((held >> 2) - row + RING) & (RING - 1)) * 4 + (held & 3)
    idx_v[...] = jnp.zeros_like(idx_v)
    idx_v[0:1, :] = jnp.where(last < 0, NNZ, last)
    idx_v[1:2, 0:NNZ] = jnp.where(before < 0, NNZ, before)
    idx_v[2:3, 0:NNZ] = slot
    to_scalars = pltpu.make_async_copy(idx_v, idx, local_sem.at[8])
    to_scalars.start()
    s[0, NNZ] = jnp.zeros((BS, BS), F32)
    s[1, NNZ] = jnp.zeros((BS, BS), F32)

    for n in range(2):
        for g in first:
            g.arrive(n)
    arrived(x.at[pl.ds(3, 3)], ag_last.at[0])
    for copy in loads[3:]:
        copy.wait()
    to_scalars.wait()

    def products(half, source):
        for e in range(NNZ):
            held = source(idx[2, e])
            s[half, e] = jnp.dot(v[e], held, preferred_element_type=F32) + s[half, idx[1, e]]

    class Pair:
        def __init__(self, number, half, j):
            self.p, self.half, self.j, self.sems = number, half, j, rs_recv.at[number]

        def own(self, w, d, g, kk):
            if w == 0:
                xx, yy = (cx + d) & 3, (cy + g) & 3
            else:
                yy, xx = (cy + d) & 3, (cx + g) & 3
            b = ((yy * 4 + xx) * 2 + kk) * 4 + self.j * 2 + w
            return s[self.half, idx[0, b]]

        def chip(self, w, d, e, g):
            return self.own(w, d, g, core) + sib_in[self.p, e, w, g].astype(F32)

        def to_sibling(self, e, d, step, n, sem):
            p = self.p
            for w in range(2):

                def body(i):
                    for g in range(4):
                        sib_out[p, e + i, w, g] = self.own(w, d + step * i, g, 1 - core).astype(BF)

                loop(n, body)
            part = pl.ds(e, n)
            send(sib_out.at[p, part], sib_in.at[p, part], SIB, self.sems.at[sem], sibling)

        def sib_far(self):
            self.to_sibling(0, 2, 0, 1, SIB_FAR)

        def sib_near(self):
            self.to_sibling(1, 1, 2, 2, SIB_NEAR)

        def sib_here(self):
            self.to_sibling(3, 0, 0, 1, SUMS)

        def far(self):
            p = self.p
            arrived(sib_in.at[p, 0], self.sems.at[SIB_FAR])
            for w in range(2):

                def body(g):
                    q[p, w, g] = self.chip(w, 2, 0, g).astype(BF)

                loop(4, body)
                for at_q, step in ((0, 1), (2, -1)):
                    part = pl.ds(at_q, 2)
                    send(q.at[p, w, part], t1.at[p, w, part], FIRST, self.sems.at[FAR], ways[w][0][step])

        def near(self):
            p = self.p
            arrived(sib_in.at[p, pl.ds(1, 2)], self.sems.at[SIB_NEAR])
            for w in range(2):

                def body(i):
                    q[p, w, 4 + i] = self.chip(w, 1 + 2 * (i // 2), 1 + i // 2, (i + 2) & 3).astype(BF)

                loop(4, body)
                for side, step in ((0, 1), (1, -1)):
                    send(
                        q.at[p, w, pl.ds(4 + 2 * side, 2)], r1.at[p, w, side, pl.ds(2 - 2 * side, 2)],
                        FIRST, self.sems.at[SUMS], ways[w][0][step],
                    )

        def passed(self):
            p = self.p
            arrived(t1.at[p], self.sems.at[FAR])
            for n, sem in ((1, SUMS), (0, LAST_SUMS)):
                for w in range(2):
                    for side, step in ((0, 1), (1, -1)):
                        g = 2 * side + n
                        held = self.chip(w, 1 + 2 * side, 1 + side, g)
                        comb[p, w, g] = (held + t1[p, w, g].astype(F32)).astype(BF)
                        send(comb.at[p, w, g], r1.at[p, w, side, g], COMB, self.sems.at[sem], ways[w][0][step])

        def sums(self, w, g):
            p = self.p
            return self.chip(w, 0, 3, g) + (r1[p, w, 0, g].astype(F32) + r1[p, w, 1, g].astype(F32))

        def away(self, w, g):
            p = self.p
            fb[p, w, g - 1] = self.sums(w, g).astype(BF)
            send(fb.at[p, w, g - 1], r2.at[p, w, g - 1], SECOND, self.sems.at[TOTAL], ways[w][1][-1 if g == 3 else g])

        def second(self):
            p = self.p
            arrived(sib_in.at[pl.ds(0, 5), 0, 0], self.sems.at[SUMS])
            for g in (1, 3):
                for w in range(2):
                    self.away(w, g)
            arrived(r1.at[p, 0, 0], self.sems.at[LAST_SUMS])
            for w in range(2):
                self.away(w, 2)
            for w in range(2):
                f[p, w] = self.sums(w, 0)

        def part_way(self, src, dst, rows, sem, step):
            send(fb.at[self.p, *src, rows], r2.at[self.p, *dst, rows], SECOND, self.sems.at[sem], ways[src[0]][1][step])

        def second_halves(self):
            p, upper, lower = self.p, pl.ds(0, 64), pl.ds(64, 64)
            arrived(sib_in.at[pl.ds(0, 5), 0, 0], self.sems.at[SUMS])
            arrived(r1.at[p, 0, 0], self.sems.at[LAST_SUMS])
            for w in range(2):
                fb[p, w, 0] = self.sums(w, 2).astype(BF)
                self.part_way((w, 0), (w, 2), upper, HALVES, 1)
                self.part_way((w, 0), (w, 2), lower, HALVES, -1)
            for w in range(2):
                fb[p, w, 1, 64:128] = self.sums(w, 1)[64:128].astype(BF)
                self.part_way((w, 1), (w, 0), lower, TOTAL, 1)
                fb[p, w, 1, 0:64] = self.sums(w, 3)[0:64].astype(BF)
                self.part_way((w, 1), (w, 1), upper, TOTAL, -1)
                f[p, w] = self.sums(w, 0)

        def third(self):
            p, upper, lower = self.p, pl.ds(0, 64), pl.ds(64, 64)
            arrived(fb.at[p, 0, pl.ds(0, 2)], self.sems.at[HALVES])
            for w in range(2):
                fb[p, w, 2, 0:64] = (self.sums(w, 1)[0:64] + r2[p, w, 2, 0:64].astype(F32)).astype(BF)
                self.part_way((w, 2), (w, 0), upper, TOTAL, 1)
                fb[p, w, 2, 64:128] = (self.sums(w, 3)[64:128] + r2[p, w, 2, 64:128].astype(F32)).astype(BF)
                self.part_way((w, 2), (w, 1), lower, TOTAL, -1)

        def total_halves(self):
            p = self.p
            arrived(r1.at[p, 0, 0], self.sems.at[TOTAL])
            return [(f[p, w] + (r2[p, w, 0].astype(F32) + r2[p, w, 1].astype(F32))).astype(BF) for w in range(2)]

        def total(self):
            p = self.p
            arrived(r2.at[p], self.sems.at[TOTAL])
            return [
                (f[p, w] + r2[p, w, 0].astype(F32) + (r2[p, w, 1].astype(F32) + r2[p, w, 2].astype(F32))).astype(BF)
                for w in range(2)
            ]

    def hidden(n, t):
        made = jnp.dot(a[n, t], w1[...], preferred_element_type=F32) + b1[...]
        made = jnp.maximum(made, 0.0).astype(BF)
        h[0, n * 4 + t] = made[:, :BS]
        h[1, n * 4 + t] = made[:, BS:]

    products(0, lambda n: x[n // 4, n % 4])
    pairs = [Pair(j, 0, j) for j in range(2)]
    gathers = [Gather(a, 1, t) for t in range(4)]

    def publish(j):
        for w, block in enumerate(pairs[j].total()):
            a[0, 2 * j + w] = block
            gathers[2 * j + w].start(0, 0)
        for w in range(2):
            hidden(0, 2 * j + w)

    def arrive(n, j):
        if n == 2:
            arrived(r2.at[0], ag_last.at[1 + j])
        filled = [(t, slot_at) for t in (2 * j, 2 * j + 1) for slot_at in gathers[t].arrive(n)]
        for t, slot_at in filled:
            hidden(slot_at, t)

    one, two = pairs
    one.sib_far()
    two.sib_far()
    one.sib_near()
    two.sib_near()
    one.sib_here()
    two.sib_here()
    one.far()
    two.far()
    one.near()
    one.passed()
    two.near()
    two.passed()
    one.second()
    two.second()
    publish(0)
    publish(1)
    for n in range(3):
        arrive(n, 0)
        arrive(n, 1)

    pairs = [Pair(2 + i, i // 2, i % 2) for i in range(4)]

    def finish(pair):
        for w, block in enumerate(pair.total() if pair in (three, four,) else pair.total_halves()):
            agg[2 * pair.j + w, :, pair.half * BS : (pair.half + 1) * BS] = block

    one, two, three, four = pairs
    products(0, lambda n: h[0, n])
    one.sib_far()
    two.sib_far()
    one.sib_near()
    two.sib_near()
    one.sib_here()
    two.sib_here()
    one.far()
    two.far()
    one.near()
    products(1, lambda n: h[1, n])
    three.sib_far()
    four.sib_far()
    one.passed()
    two.near()
    three.far()
    three.sib_near()
    four.sib_near()
    three.sib_here()
    four.sib_here()
    two.passed()
    three.near()
    four.far()
    three.passed()
    four.near()
    four.passed()
    one.second_halves()
    two.second_halves()
    three.second()
    one.third()
    four.second()
    two.third()
    finish(one)
    finish(two)

    def put(t):
        made = jnp.dot(agg[t], w2[...], preferred_element_type=F32) + b2[...]
        out[t] = jnp.maximum(made, 0.0).astype(BF)

    finish(three)
    put(0)
    put(1)
    finish(four)
    put(2)
    put(3)
    all_sent(sib_out, SIB)
    all_sent(q, FIRST)
    all_sent(comb, COMB)
    all_sent(fb, SECOND)
    all_sent(x.at[pl.ds(1, 7)], GATHER1)
    all_sent(a.at[pl.ds(1, 7)], GATHER2)


def local(features, block_rows, block_cols, block_values, weight_one, bias_one, weight_two, bias_two):
    block = (BS, BS)
    return pl.pallas_call(
        kernel,
        out_shape=pltpu.VMEM((4, BS, 2 * BS), BF),
        in_specs=[pl.BlockSpec(memory_space=pl.ANY)] * 8,
        out_specs=pl.BlockSpec(memory_space=pltpu.VMEM),
        scratch_shapes=[
            pltpu.VMEM((NNZ, *block), BF),
            pltpu.VMEM((RING, 4, *block), BF),
            pltpu.VMEM((RING, 4, *block), BF),
            pltpu.VMEM((2, RING * 4, *block), BF),
            pltpu.VMEM((2, NNZ + 1, *block), F32),
            pltpu.VMEM((4, BS, 2 * BS), BF),
            pltpu.VMEM((128, 256), BF),
            pltpu.VMEM((1, 256), F32),
            pltpu.VMEM((256, 256), BF),
            pltpu.VMEM((1, 256), F32),
            pltpu.VMEM((1, NNZ), jnp.int32),
            pltpu.VMEM((1, NNZ), jnp.int32),
            pltpu.VMEM((8, BS), jnp.int32),
            pltpu.SMEM((8, BS), jnp.int32),
            pltpu.VMEM((PAIRS, 4, 2, 4, *block), BF),
            pltpu.VMEM((PAIRS, 4, 2, 4, *block), BF),
            pltpu.VMEM((PAIRS, 2, 8, *block), BF),
            pltpu.VMEM((PAIRS, 2, 4, *block), BF),
            pltpu.VMEM((PAIRS, 2, 4, *block), BF),
            pltpu.VMEM((PAIRS, 2, 2, 4, *block), BF),
            pltpu.VMEM((PAIRS, 2, *block), F32),
            pltpu.VMEM((PAIRS, 2, 3, *block), BF),
            pltpu.VMEM((PAIRS, 2, 3, *block), BF),
            pltpu.SemaphoreType.DMA((6,)),
            pltpu.SemaphoreType.DMA((PAIRS, 7)),
            pltpu.SemaphoreType.DMA((8, 4)),
            pltpu.SemaphoreType.DMA((3,)),
            pltpu.SemaphoreType.DMA((9,)),
        ],
        compiler_params=pltpu.CompilerParams(
            collective_id=1, has_side_effects=True, vmem_limit_bytes=56 * 2**20
        ),
        name="two_layers",
    )(
        features.reshape(4, *block),
        block_rows.reshape(1, NNZ),
        block_cols.reshape(1, NNZ),
        block_values.reshape(NNZ, *block),
        weight_one,
        bias_one.reshape(1, -1),
        weight_two,
        bias_two.reshape(1, -1),
    ).reshape(512, 256)


def solution(mesh):
    placed = (
        P(("row", "col"), None),
        P("row", "col", None),
        P("row", "col", None),
        P("row", "col", None, None, None),
        P(),
        P(),
        P(),
        P(),
    )
    return jax.shard_map(
        local, mesh=mesh, in_specs=placed, out_specs=P(("row", "col"), None), check_vma=False
    )
```
